512 devices in a mesh: gx: 64 (over x, z), gy: 8 (over y, core).
Axes of the slice: x: 4, y: 4, z: 16, core: 2. Of those that a mesh axis runs over, the one named last changes fastest.
Arguments:
- snapshot: bfloat16 [3, 512, 128, 1024], P(None, 'gx', 'gy'), may hold values from -6 to 6
- basis: bfloat16 [3, 64, 16, 128, 512], P(None, 'gx', 'gy'), may hold values from -3000 to 3000
- taps: bfloat16 [3, 17], replicated, may hold values from 0.099609375 to 1
Outputs:
- new_modes: bfloat16 [3, 64, 16, 128, 512], P(None, 'gx', 'gy')
- new_mode: float32 [3, 64, 16, 128], P(None, 'gx', 'gy')
- factor: float32 [513, 513], replicated
The draws below stay inside these ranges and needn't reach their ends.
All inputs are finite; a program needn't handle non-finite values.
Results may differ from the reference program's by a relative error of at most 0.0012.
The reference program's roundings to bfloat16 on the way (of `filtered` and `stack`) count: a program that leaves them out, or rounds other values in their place, can miss the bound.
Values sent between devices are 32-bit elements; how exact they have to be, the bound alone decides.
A program may use at most 64 MiB of HBM per device.

```python
import math
import jax
import jax.numpy as jnp
from jax import lax

K = 512
STRIDE = 8
TAPS = 17
NZ = 1024
FZ = 128
NX = 512
NY = 128
NFX = 64
NFY = 16


def draw_basis(key, part):
    key_base = jax.random.fold_in(key, 11)
    key_rows = jax.random.fold_in(key, 12)
    key_cols = jax.random.fold_in(key, 13)
    key_pair = jax.random.fold_in(key, 14)
    key_mixing = jax.random.fold_in(key, 15)
    total = 3 * NFX * NFY * FZ
    base = jax.random.normal(key_base, (total, K), jnp.float32)
    mixing = jnp.eye(K, dtype=jnp.float32) + 0.6 * jax.random.normal(key_mixing, (K, K), jnp.float32) / math.sqrt(K)
    mixed = jnp.dot(base, mixing, precision=lax.Precision.HIGHEST)
    row_scale = jnp.exp(jax.random.uniform(key_rows, (total, 1), jnp.float32, 0.0, math.log(10.0)))
    col_scale = jnp.exp(jax.random.uniform(key_cols, (1, K), jnp.float32, 0.0, math.log(10.0)))
    slab = jnp.arange(total, dtype=jnp.int32) // (NFY * FZ) % NFX
    owner = jax.random.permutation(key_pair, NFX)
    column_slab = owner[jnp.arange(K, dtype=jnp.int32) * NFX // K]
    spike = jnp.where(slab[:, None] == column_slab[None, :], 4.0, 1.0)
    values = mixed * spike
    values = values * row_scale * col_scale
    return values.reshape(3, NFX, NFY, FZ, K).astype(jnp.bfloat16)


def shard_levels(key, shape, cuts, smallest, largest):
    factor_of = 1.0
    for dim, shards_of in cuts:
        steps = jax.random.uniform(jax.random.fold_in(jax.random.fold_in(key, 6), dim), (shards_of,), jnp.float32, smallest / len(cuts), largest / len(cuts))
        factor_of = factor_of * jnp.repeat(jnp.exp(steps), shape[dim] // shards_of).reshape((-1,) + (1,) * (len(shape) - 1 - dim))
    return factor_of


def normal_values(own_key, shape, scale, limit, cuts=(), held_as=jnp.bfloat16):
    level = shard_levels(own_key, shape, cuts, -0.22, 0.18) if cuts else 1.0
    values = jax.random.normal(own_key, shape, jnp.float32) * scale * level
    return jnp.minimum(jnp.maximum(values, -limit), limit).astype(held_as)


def setup_inputs(seed: int = 0) -> dict:
    key_list = jax.random.split(jax.random.key(seed), 4)
    return {
        "snapshot": normal_values(key_list[0], (3, NX, NY, NZ), 1.0, 6.0, ((1, 64), (2, 8))),
        "basis": draw_basis(jax.random.fold_in(key_list[3], 71), 0),
        "taps": jnp.clip(jax.random.uniform(key_list[2], (3, TAPS), jnp.float32, 0.099609375, 1.0), 0.099609375, 1.0).astype(jnp.bfloat16),
    }


def band(taps_row, length, out_len, shift, wrap):
    rows = jnp.arange(length, dtype=jnp.int32)[:, None]
    cols = jnp.arange(out_len, dtype=jnp.int32)[None, :]
    lag = rows - STRIDE * cols + shift
    if wrap:
        lag = lag % length
    hits = lag[:, :, None] == jnp.arange(2 * STRIDE + 1, dtype=jnp.int32)[None, None, :]
    return jnp.sum(jnp.where(hits, taps_row[None, None, :], jnp.zeros((), taps_row.dtype)), axis=-1).astype(taps_row.dtype)

def reference(snapshot, basis, taps):
    comps, cells_x, cells_y, cells_z = snapshot.shape
    matrix_z = band(taps[2], cells_z, cells_z // STRIDE, STRIDE, True)
    along_z = jnp.dot(snapshot.reshape(-1, cells_z).astype(jnp.float32), matrix_z.astype(jnp.float32), preferred_element_type=jnp.float32)
    along_z = along_z.reshape(comps, cells_x, cells_y, cells_z // STRIDE)
    matrix_y = band(taps[1], cells_y, cells_y // STRIDE, STRIDE, False).astype(jnp.float32)
    along_y = jnp.einsum('cxyz,yf->cxfz', along_z, matrix_y, precision=lax.Precision.HIGHEST)
    matrix_x = band(taps[0], cells_x, cells_x // STRIDE, STRIDE, True).astype(jnp.float32)
    along_x = jnp.einsum('cxyz,xf->cfyz', along_y, matrix_x, precision=lax.Precision.HIGHEST)
    filtered = along_x.astype(jnp.bfloat16).reshape(-1)
    modes = basis.shape[-1]
    stack = jnp.concatenate([basis.reshape(-1, modes), filtered[:, None]], axis=1)
    total = stack.shape[0]
    gram = jnp.einsum('rk,rj->kj', stack.astype(jnp.float32), stack.astype(jnp.float32), preferred_element_type=jnp.float32) / total
    lower = jnp.linalg.cholesky(gram)
    solved = lax.linalg.triangular_solve(lower, stack.astype(jnp.float32), left_side=False, lower=True, transpose_a=True)
    new_modes = solved[:, :modes].astype(jnp.bfloat16).reshape(basis.shape)
    new_mode = solved[:, modes].reshape(basis.shape[:-1])
    return (new_modes, new_mode, lower.T)
```

```python
import functools
import jax, jax.numpy as jnp
from jax import lax
from jax.sharding import PartitionSpec as P
from jax.experimental import pallas as pl
from jax.experimental.pallas import tpu as pltpu

F32, BF16 = jnp.float32, jnp.bfloat16
B = 128
HI = lax.Precision.HIGHEST

def lane_splat(tile, lane):
    return jnp.broadcast_to(tile[:, lane:lane + 1], (8, B))

def row_splat(tile, row):
    return jnp.broadcast_to(tile[row:row + 1, :], (8, B))

def recip(x):
    r = pl.reciprocal(x, approx=True)
    r = r * (2.0 - x * r)
    return r

def factor_block(a):
    sub = lax.broadcasted_iota(jnp.int32, (8, B), 0)
    lane = lax.broadcasted_iota(jnp.int32, (8, B), 1)
    n = B // 8
    a = list(a)
    z = [jnp.where(lane == 8 * t + sub, 1.0, 0.0) for t in range(n)]
    diag = [lane_splat(a[0], j) for j in range(8)]
    for p in range(n):
        cols = diag
        inv = []
        row = {}
        pivots = jnp.ones((8, B), F32)
        for k in range(8):
            pivot = row_splat(cols[k], k)
            pivots = jnp.where(sub == k, pivot, pivots)
            r = recip(pivot)
            inv.append(r)
            m = jnp.where(sub > k, cols[k] * r, 0.0)
            for j in range(k + 1, 8):
                row[k, j] = row_splat(cols[j], k)
                cols[j] = cols[j] - m * row[k, j]
            if k < 7:
                a[p] = a[p] - m * row_splat(a[p], k)
                z[p] = z[p] - m * row_splat(z[p], k)
        mult = {}
        for t in range(p + 1, n):
            c = [lane_splat(a[t], 8 * p + j) for j in range(8)]
            for k in range(8):
                m = c[k] * inv[k]
                mult[t, k] = m
                for j in range(k + 1, 8):
                    c[j] = c[j] - m * row[k, j]
            if t == p + 1:
                diag = []
                for j in range(8):
                    d = lane_splat(a[t], 8 * t + j)
                    for k in range(8):
                        d = d - mult[t, k] * row_splat(c[k], j)
                    diag.append(d)
        for k in range(8):
            if p + 1 < n:
                ua, uz = row_splat(a[p], k), row_splat(z[p], k)
            for t in range(p + 1, n):
                a[t] = a[t] - mult[t, k] * ua
                z[t] = z[t] - mult[t, k] * uz
        s = lax.rsqrt(pivots)
        a[p] = jnp.where(lane >= 8 * p + sub, a[p] * s, 0.0)
        z[p] = z[p] * s
    return a, z

PAIRS = [(b, c) for b in range(4) for c in range(b, 4)]
INDEX = {pair: i for i, pair in enumerate(PAIRS)}

def nn(x, y): return lax.dot_general(x, y, (((1,), (0,)), ((), ())), precision=HI, preferred_element_type=F32)
def tn(x, y): return lax.dot_general(x, y, (((0,), (0,)), ((), ())), precision=HI, preferred_element_type=F32)
def nt(x, y): return lax.dot_general(x, y, (((1,), (1,)), ((), ())), precision=HI, preferred_element_type=F32)
def nt16(x, y): return lax.dot_general(x, y, (((1,), (1,)), ((), ())), preferred_element_type=F32)

def split(x):
    hi = x.astype(BF16)
    return hi, (x - hi.astype(F32)).astype(BF16)

def k2_kernel(total, nblk, g_ref, f_ref, basis_ref, modes_ref, mode_ref, factor_ref, s_ref, zw_ref, zh_ref, zl_ref):
    scale = 1.0 / total
    for i in range(10):
        s_ref[i] = g_ref[i * B:(i + 1) * B, :] * scale
    grow = g_ref[1280:1288, :] * scale
    factor_ref[...] = jnp.zeros_like(factor_ref)
    zh_ref[...] = jnp.zeros_like(zh_ref)
    zl_ref[...] = jnp.zeros_like(zl_ref)
    zw_ref[...] = jnp.zeros_like(zw_ref)
    for b in range(nblk):
        blk = INDEX[b, b]
        a, z = factor_block([s_ref[blk, 8 * t:8 * t + 8, :] for t in range(16)])
        w = jnp.concatenate(z, axis=0)
        lo = b * B
        factor_ref[lo:lo + B, lo:lo + B] = jnp.concatenate(a, axis=0)
        zw_ref[lo:lo + B, lo:lo + B] = w
        r = {}
        for c in range(b + 1, 4):
            r[c] = nn(w, s_ref[INDEX[b, c]])
            factor_ref[lo:lo + B, c * B:(c + 1) * B] = r[c]
        if b:
            zw_ref[lo:lo + B, 0:lo] = nn(w, zw_ref[lo:lo + B, 0:lo])
        zrow = zw_ref[lo:lo + B, 0:lo + B]
        for i in range(b + 1, 4):
            for c in range(i, 4):
                s_ref[INDEX[i, c]] = s_ref[INDEX[i, c]] - tn(r[i], r[c])
            zw_ref[i * B:(i + 1) * B, 0:lo + B] = zw_ref[i * B:(i + 1) * B, 0:lo + B] - tn(r[i], zrow)
        zh, zl = split(zrow)
        zh_ref[lo:lo + B, 0:lo + B] = zh
        zl_ref[lo:lo + B, 0:lo + B] = zl
        out = nt16(basis_ref[:, 0:lo + B], zh_ref[lo:lo + B, 0:lo + B]) + nt16(basis_ref[:, 0:lo + B], zl_ref[lo:lo + B, 0:lo + B])
        modes_ref[:, lo:lo + B] = out.astype(BF16)
    g4 = jnp.concatenate([grow[i:i + 1, :] for i in range(4)], axis=1)
    g8 = jnp.broadcast_to(g4, (8, 512))
    zall = zw_ref[...]
    rcol = nt(zall, g8)
    rrow = nt(g8, zall)
    v = nn(rrow, zall)
    d2 = grow[4:5, 0:1] - jnp.sum(rrow[0:1] * rrow[0:1], axis=1, keepdims=True)
    inv_d = lax.rsqrt(d2)
    factor_ref[0:512, 512:513] = rcol[:, 0:1]
    factor_ref[512:513, 512:513] = d2 * inv_d
    vh, vl = split(v)
    y = nt16(vh, basis_ref[...]) + nt16(vl, basis_ref[...])
    y6 = jnp.concatenate([y[0:1, i * B:(i + 1) * B] for i in range(6)], axis=0)
    mode_ref[...] = (f_ref[...] - y6) * inv_d

def k2(g, f, basis, total=393216.0, nblk=4, kern=k2_kernel):
    rows = basis.shape[0]
    return pl.pallas_call(
        functools.partial(kern, total, nblk),
        out_shape=(jax.ShapeDtypeStruct((rows, 512), BF16), jax.ShapeDtypeStruct((6, B), F32), jax.ShapeDtypeStruct((513, 513), F32)),
        in_specs=[pl.BlockSpec(memory_space=pltpu.VMEM)] * 3,
        out_specs=[pl.BlockSpec(memory_space=pltpu.VMEM)] * 3,
        scratch_shapes=[pltpu.VMEM((10, B, B), F32), pltpu.VMEM((512, 512), F32), pltpu.VMEM((512, 512), BF16), pltpu.VMEM((512, 512), BF16)],
        compiler_params=pltpu.CompilerParams(vmem_limit_bytes=40 << 20),
        name="factor",
    )(g, f, basis)

MESH = pl.DeviceIdType.MESH
NPLANE, NZR, CH = 16, 16, 48
PIECE = CH // NZR
ROWS = 2 * NPLANE * CH
NEAR = [(dx, dy) for dx in (0, 1, -1) for dy in (0, 1, -1) if (dx, dy) != (0, 0)]


def tap_tiles(taps, d, sub):
    def at(i):
        return jnp.broadcast_to(taps[d:d + 1, i:i + 1], (8, B))
    ahead = behind = jnp.zeros((8, B), F32)
    for s in range(8):
        ahead = jnp.where(sub == s, at(8 + s), ahead)
        behind = jnp.where(sub == s, at(s), behind)
    return ahead, behind, jnp.where(sub == 0, at(16), 0.0)


def reduce_kernel(taps_ref, snap_ref, basis_ref, gram_ref, filt_ref, band_ref, near_out, near_in, acc, recv_a, recv_b, chunk_ref, recv_c, piece_ref, ring_ref, full_ref, near_s, near_r, sa, ra, sb, rb, sc, rc, sd, rd, se, re, sf, rf):
    gx, gy = lax.axis_index("gx"), lax.axis_index("gy")
    x, z = gx // NZR, gx % NZR
    y, core = gy // 2, gy % 2
    plane = x * 4 + y

    def near_id(dx, dy):
        return ((gx + dx + 64) % 64, (gy + dy + 8) % 8)

    def plane_id(k):
        p = (plane + k) % NPLANE
        return ((p // 4) * NZR + z, (p % 4) * 2 + core)

    def z_id(k):
        return (x * NZR + (z + k) % NZR, gy)

    sibling = (gx, y * 2 + (1 - core))
    barrier = pltpu.get_barrier_semaphore()
    partners = [near_id(dx, dy) for dx, dy in NEAR] + [plane_id(k) for k in range(1, NPLANE)] + [z_id(k) for k in range(1, NZR)] + [sibling]
    for partner in partners:
        pl.semaphore_signal(barrier, inc=1, device_id=partner, device_id_type=MESH)

    sub = lax.broadcasted_iota(jnp.int32, (8, B), 0)
    lane = lax.broadcasted_iota(jnp.int32, (8, B), 1)
    taps = taps_ref[...].astype(F32)
    ahead, behind, last = tap_tiles(taps, 2, sub)
    for m in range(0, 128, 2):
        pair = []
        for t in (m, m + 1):
            tile = jnp.where(lane == t, ahead, 0.0)
            tile = jnp.where(lane == (t + 1) % 128, behind, tile)
            pair.append(jnp.where(lane == (t + 127) % 128, last, tile))
        band_ref[8 * m:8 * m + 16, :] = jnp.concatenate(pair, axis=0).astype(BF16)
    along_z = jnp.dot(snap_ref[...], band_ref[...], preferred_element_type=F32)
    ahead, behind, last = tap_tiles(taps, 0, sub)
    w_ahead = [row_splat(ahead, s) for s in range(8)]
    w_behind = [row_splat(behind, s) for s in range(8)]
    w_last = row_splat(last, 0)
    ahead, behind, last = tap_tiles(taps, 1, sub)
    sums = {}
    for dx in (0, 1, -1):
        for dy in (0, 1, -1):
            sums[dx, dy] = jnp.zeros((8, B), F32)
    for c in range(3):
        cell = [[along_z[(c * 8 + i) * 16 + 8 * h:(c * 8 + i) * 16 + 8 * h + 8, :] for i in range(8)] for h in range(2)]
        for dx in (0, 1, -1):
            half = []
            for h in range(2):
                if dx == -1:
                    half.append(w_last * cell[h][0])
                else:
                    w = w_ahead if dx == 0 else w_behind
                    v = w[0] * cell[h][0]
                    for i in range(1, 8):
                        v = v + w[i] * cell[h][i]
                    half.append(v)
            def put(dy, q, tile):
                total = jnp.sum(tile, axis=0, keepdims=True)
                sums[dx, dy] = jnp.where(sub == 2 * c + q, jnp.broadcast_to(total, (8, B)), sums[dx, dy])
            put(0, 0, ahead * half[0] + last * half[1])
            put(0, 1, behind * half[0] + ahead * half[1])
            put(1, 0, behind * half[1])
            put(-1, 1, last * half[0])
    for e, (dx, dy) in enumerate(NEAR):
        tile = sums[dx, dy]
        if dy == 1:
            tile = jnp.where(gy == 7, 0.0, tile)
        if dy == -1:
            tile = jnp.where(gy == 0, 0.0, tile)
        near_out[e] = tile
    pl.semaphore_wait(barrier, len(partners))

    def copy(src, dst, ssem, rsem, device):
        c = pltpu.make_async_remote_copy(src_ref=src, dst_ref=dst, send_sem=ssem, recv_sem=rsem, device_id=device, device_id_type=MESH)
        c.start()
        return c

    near = [copy(near_out.at[e], near_in.at[e], near_s.at[e], near_r.at[e], near_id(dx, dy)) for e, (dx, dy) in enumerate(NEAR)]

    at = 0
    for b in range(4):
        width = 512 - b * B
        part = lax.dot_general(basis_ref[:, b * B:(b + 1) * B], basis_ref[:, b * B:512], (((0,), (0,)), ((), ())), preferred_element_type=F32)
        for c in range(width // B):
            acc[at:at + B, :] = part[:, c * B:(c + 1) * B]
            at += B

    for c in near:
        c.wait()
    f = sums[0, 0]
    for e in range(len(NEAR)):
        f = f + near_in[e]
    f16 = f.astype(BF16)
    f = f16.astype(F32)
    filt_ref[...] = f[0:6, :]
    frow = jnp.concatenate([jnp.broadcast_to(f[i:i + 1, :], (8, B)) for i in range(6)], axis=1).astype(BF16)
    g = jnp.dot(frow, basis_ref[...], preferred_element_type=F32)
    sq = jnp.where(sub < 6, f * f, 0.0)
    ff = jnp.sum(jnp.sum(sq, axis=1, keepdims=True), axis=0, keepdims=True)
    tail = jnp.where(sub == 4, jnp.broadcast_to(ff, (8, B)), 0.0)
    for i in range(4):
        tail = jnp.where(sub == i, g[:, i * B:(i + 1) * B], tail)
    acc[1280:1288, :] = tail
    acc[1288:ROWS, :] = jnp.zeros((ROWS - 1288, B), F32)

    half = NPLANE * CH
    ca = copy(acc.at[pl.ds((1 - core) * half, half)], recv_a, sa, ra, sibling)
    ca.wait()
    recv_a[...] = recv_a[...] + acc[pl.ds(core * half, half), :]
    cb = []
    for k in range(1, NPLANE):
        p = (plane + k) % NPLANE
        cb.append(copy(recv_a.at[pl.ds(p * CH, CH)], recv_b.at[k - 1], sb.at[k - 1], rb.at[k - 1], plane_id(k)))
    total = recv_a[pl.ds(plane * CH, CH), :]
    for k in range(1, NPLANE):
        cb[k - 1].wait_recv()
        total = total + recv_b[k - 1]
    for i in range(NZR):
        chunk_ref[i] = total[i * PIECE:(i + 1) * PIECE, :]
    cc = []
    for k in range(1, NZR):
        cc.append(copy(chunk_ref.at[(z + k) % NZR], recv_c.at[k - 1], sc.at[k - 1], rc.at[k - 1], z_id(k)))
    total = chunk_ref[z]
    for k in range(1, NZR):
        cc[k - 1].wait_recv()
        total = total + recv_c[k - 1]
    piece_ref[...] = total
    cd = []
    for k in range(1, NZR):
        cd.append(copy(piece_ref, ring_ref.at[z], sd.at[k - 1], rd.at[k - 1], z_id(k)))
    ring_ref[z] = total
    for k in range(1, NZR):
        cd[k - 1].wait_recv()
    mine = recv_a.at[pl.ds(0, CH)]
    for c in cb:
        c.wait_send()
    for i in range(NZR):
        recv_a[i * PIECE:(i + 1) * PIECE, :] = ring_ref[i]
    ce = []
    for k in range(1, NPLANE):
        ce.append(copy(mine, full_ref.at[core, plane], se.at[k - 1], re.at[k - 1], plane_id(k)))
    full_ref[core, plane] = recv_a[0:CH, :]
    cf = [copy(mine, full_ref.at[core, plane], sf.at[0], rf.at[0], sibling)]
    for k in range(1, NPLANE):
        ce[k - 1].wait_recv()
        p = (plane - k + NPLANE) % NPLANE
        cf.append(copy(full_ref.at[core, p], full_ref.at[core, p], sf.at[k], rf.at[k], sibling))
    for c in cf:
        c.wait_recv()
    for i in range(2):
        for j in range(NPLANE):
            gram_ref[(i * NPLANE + j) * CH:(i * NPLANE + j + 1) * CH, :] = full_ref[i, j]
    for c in cc + cd + ce + cf:
        c.wait_send()


def reduced(taps, snap, basis):
    dma = pltpu.SemaphoreType.DMA
    return pl.pallas_call(
        reduce_kernel,
        out_shape=(jax.ShapeDtypeStruct((ROWS, B), F32), jax.ShapeDtypeStruct((6, B), F32)),
        in_specs=[pl.BlockSpec(memory_space=pltpu.VMEM)] * 3,
        out_specs=[pl.BlockSpec(memory_space=pltpu.VMEM)] * 2,
        scratch_shapes=[
            pltpu.VMEM((1024, B), BF16),
            pltpu.VMEM((8, 8, B), F32),
            pltpu.VMEM((8, 8, B), F32),
            pltpu.VMEM((ROWS, B), F32),
            pltpu.VMEM((NPLANE * CH, B), F32),
            pltpu.VMEM((NPLANE - 1, CH, B), F32),
            pltpu.VMEM((NZR, PIECE, B), F32),
            pltpu.VMEM((NZR - 1, PIECE, B), F32),
            pltpu.VMEM((PIECE, B), F32),
            pltpu.VMEM((NZR, PIECE, B), F32),
            pltpu.VMEM((2, NPLANE, CH, B), F32),
            dma((8,)), dma((8,)), dma, dma,
            dma((15,)), dma((15,)), dma((15,)), dma((15,)), dma((15,)), dma((15,)), dma((15,)), dma((15,)), dma((16,)), dma((16,)),
        ],
        compiler_params=pltpu.CompilerParams(vmem_limit_bytes=40 << 20, collective_id=0, has_side_effects=True),
        name="reduce",
    )(taps, snap, basis)


def local(snapshot, basis, taps):
    flat = basis.reshape(-1, basis.shape[-1])
    g, f = reduced(taps, snapshot.reshape(-1, snapshot.shape[-1]), flat)
    total = flat.shape[0] * lax.axis_size("gx") * lax.axis_size("gy")
    modes, mode, fac = k2(g, f, flat, float(total))
    return modes.reshape(basis.shape), mode.reshape(basis.shape[:-1]), fac


def solution(mesh):
    in_specs = (P(None, "gx", "gy", None), P(None, "gx", "gy", None, None), P())
    out_specs = (P(None, "gx", "gy", None, None), P(None, "gx", "gy", None), P())
    return jax.shard_map(local, mesh=mesh, in_specs=in_specs, out_specs=out_specs, check_vma=False)
```

```python
import functools
import jax, jax.numpy as jnp
from jax import lax
from jax.sharding import PartitionSpec as P
from jax.experimental import pallas as pl
from jax.experimental.pallas import tpu as pltpu

F32, BF16 = jnp.float32, jnp.bfloat16
B = 128
HI = lax.Precision.HIGHEST

def lane_splat(tile, lane):
    return jnp.broadcast_to(tile[:, lane:lane + 1], (8, B))

def row_splat(tile, row):
    return jnp.broadcast_to(tile[row:row + 1, :], (8, B))

def recip(x):
    r = pl.reciprocal(x, approx=True)
    r = r * (2.0 - x * r)
    return r

def factor_block(a):
    sub = lax.broadcasted_iota(jnp.int32, (8, B), 0)
    lane = lax.broadcasted_iota(jnp.int32, (8, B), 1)
    n = B // 8
    a = list(a)
    z = [jnp.where(lane == 8 * t + sub, 1.0, 0.0) for t in range(n)]
    diag = [lane_splat(a[0], j) for j in range(8)]
    for p in range(n):
        cols = diag
        inv = []
        row = {}
        pivots = jnp.ones((8, B), F32)
        for k in range(8):
            pivot = row_splat(cols[k], k)
            pivots = jnp.where(sub == k, pivot, pivots)
            r = recip(pivot)
            inv.append(r)
            m = jnp.where(sub > k, cols[k] * r, 0.0)
            for j in range(k + 1, 8):
                row[k, j] = row_splat(cols[j], k)
                cols[j] = cols[j] - m * row[k, j]
            if k < 7:
                a[p] = a[p] - m * row_splat(a[p], k)
                z[p] = z[p] - m * row_splat(z[p], k)
        mult = {}
        for t in range(p + 1, n):
            c = [lane_splat(a[t], 8 * p + j) for j in range(8)]
            for k in range(8):
                m = c[k] * inv[k]
                mult[t, k] = m
                for j in range(k + 1, 8):
                    c[j] = c[j] - m * row[k, j]
            if t == p + 1:
                diag = []
                for j in range(8):
                    d = lane_splat(a[t], 8 * t + j)
                    for k in range(8):
                        d = d - mult[t, k] * row_splat(c[k], j)
                    diag.append(d)
        for k in range(8):
            if p + 1 < n:
                ua, uz = row_splat(a[p], k), row_splat(z[p], k)
            for t in range(p + 1, n):
                a[t] = a[t] - mult[t, k] * ua
                z[t] = z[t] - mult[t, k] * uz
        s = lax.rsqrt(pivots)
        a[p] = jnp.where(lane >= 8 * p + sub, a[p] * s, 0.0)
        z[p] = z[p] * s
    return a, z

PAIRS = [(b, c) for b in range(4) for c in range(b, 4)]
INDEX = {pair: i for i, pair in enumerate(PAIRS)}

def nn(x, y): return lax.dot_general(x, y, (((1,), (0,)), ((), ())), precision=HI, preferred_element_type=F32)
def tn(x, y): return lax.dot_general(x, y, (((0,), (0,)), ((), ())), precision=HI, preferred_element_type=F32)
def nt(x, y): return lax.dot_general(x, y, (((1,), (1,)), ((), ())), precision=HI, preferred_element_type=F32)
def nt16(x, y): return lax.dot_general(x, y, (((1,), (1,)), ((), ())), preferred_element_type=F32)

def split(x):
    hi = x.astype(BF16)
    return hi, (x - hi.astype(F32)).astype(BF16)

def k2_kernel(total, nblk, g_ref, col_ref, f_ref, basis_hbm, modes_ref, mode_ref, factor_ref, s_ref, zw_ref, zh_ref, zl_ref, basis_ref, load_s):
    load = pltpu.make_async_copy(basis_hbm, basis_ref, load_s)
    load.start()
    scale = 1.0 / total
    for i in range(160):
        s_ref[i // 16, 8 * (i % 16):8 * (i % 16) + 8, :] = g_ref[i // 5, 8 * (i % 5):8 * (i % 5) + 8, :] * scale
    grow = [col_ref[i:i + 1, :] * scale for i in range(5)]
    factor_ref[...] = jnp.zeros_like(factor_ref)
    zh_ref[...] = jnp.zeros_like(zh_ref)
    zl_ref[...] = jnp.zeros_like(zl_ref)
    zw_ref[...] = jnp.zeros_like(zw_ref)
    for b in range(nblk):
        blk = INDEX[b, b]
        a, z = factor_block([s_ref[blk, 8 * t:8 * t + 8, :] for t in range(16)])
        w = jnp.concatenate(z, axis=0)
        lo = b * B
        factor_ref[lo:lo + B, lo:lo + B] = jnp.concatenate(a, axis=0)
        zw_ref[lo:lo + B, lo:lo + B] = w
        r = {}
        for c in range(b + 1, 4):
            r[c] = nn(w, s_ref[INDEX[b, c]])
            factor_ref[lo:lo + B, c * B:(c + 1) * B] = r[c]
        if b:
            zw_ref[lo:lo + B, 0:lo] = nn(w, zw_ref[lo:lo + B, 0:lo])
        zrow = zw_ref[lo:lo + B, 0:lo + B]
        for i in range(b + 1, 4):
            for c in range(i, 4):
                s_ref[INDEX[i, c]] = s_ref[INDEX[i, c]] - tn(r[i], r[c])
            zw_ref[i * B:(i + 1) * B, 0:lo + B] = zw_ref[i * B:(i + 1) * B, 0:lo + B] - tn(r[i], zrow)
        zh, zl = split(zrow)
        if b == 0:
            load.wait()
        zh_ref[lo:lo + B, 0:lo + B] = zh
        zl_ref[lo:lo + B, 0:lo + B] = zl
        out = nt16(basis_ref[:, 0:lo + B], zh_ref[lo:lo + B, 0:lo + B]) + nt16(basis_ref[:, 0:lo + B], zl_ref[lo:lo + B, 0:lo + B])
        modes_ref[:, lo:lo + B] = out.astype(BF16)
    g4 = jnp.concatenate(grow[:4], axis=1)
    g8 = jnp.broadcast_to(g4, (8, 512))
    zall = zw_ref[...]
    rcol = nt(zall, g8)
    rrow = nt(g8, zall)
    v = nn(rrow, zall)
    d2 = grow[4][:, 0:1] - jnp.sum(rrow[0:1] * rrow[0:1], axis=1, keepdims=True)
    inv_d = lax.rsqrt(d2)
    factor_ref[0:512, 512:513] = rcol[:, 0:1]
    factor_ref[512:513, 512:513] = d2 * inv_d
    vh, vl = split(v)
    y = nt16(vh, basis_ref[...]) + nt16(vl, basis_ref[...])
    y6 = jnp.concatenate([y[0:1, i * B:(i + 1) * B] for i in range(6)], axis=0)
    mode_ref[...] = (f_ref[...] - y6) * inv_d

def k2(g, col, f, basis, total=393216.0, nblk=4, kern=k2_kernel):
    rows = basis.shape[0]
    return pl.pallas_call(
        functools.partial(kern, total, nblk),
        out_shape=(jax.ShapeDtypeStruct((rows, 512), BF16), jax.ShapeDtypeStruct((6, B), F32), jax.ShapeDtypeStruct((513, 513), F32)),
        in_specs=[pl.BlockSpec(memory_space=pltpu.VMEM)] * 3 + [pl.BlockSpec(memory_space=pltpu.HBM)],
        out_specs=[pl.BlockSpec(memory_space=pltpu.VMEM)] * 3,
        scratch_shapes=[pltpu.VMEM((10, B, B), F32), pltpu.VMEM((512, 512), F32), pltpu.VMEM((512, 512), BF16), pltpu.VMEM((512, 512), BF16), pltpu.VMEM((768, 512), BF16), pltpu.SemaphoreType.DMA],
        compiler_params=pltpu.CompilerParams(vmem_limit_bytes=40 << 20),
        name="factor",
    )(g, col, f, basis)

MESH = pl.DeviceIdType.MESH
NPLANE, NZR, CH, CG = 16, 16, 48, 40
PIECE = CH // NZR
NEAR = [(dx, dy) for dx in (0, 1, -1) for dy in (0, 1, -1) if (dx, dy) != (0, 0)]
AROUND = sorted(((dx, dy) for dx in range(4) for dy in range(4) if dx or dy), key=lambda o: -(min(o[0], 4 - o[0]) + min(o[1], 4 - o[1])))
ALONG = sorted(range(1, NZR), key=lambda k: -min(k, NZR - k))


def tap_tiles(taps, d, sub):
    def at(i):
        return jnp.broadcast_to(taps[d:d + 1, i:i + 1], (8, B))
    ahead = behind = jnp.zeros((8, B), F32)
    for s in range(8):
        ahead = jnp.where(sub == s, at(8 + s), ahead)
        behind = jnp.where(sub == s, at(s), behind)
    return ahead, behind, jnp.where(sub == 0, at(16), 0.0)


def reduce_kernel(taps_hbm, snap_hbm, basis_hbm, full_ref, col_ref, filt_ref, taps_ref, snap_ref, basis_ref, band_ref, near_out, near_in, acc, recv_a, recv_b, chunk_ref, recv_c, piece_ref, ring_ref, whole_ref, gsend, grecv, gsib, gin, gout, gz, load_s, near_s, near_r, sa, ra, sb, rb, sc, rc, sd, rd, se, re, sf, rf, sga, rga, sgb, rgb, sgc, rgc, far):
    gx, gy = lax.axis_index("gx"), lax.axis_index("gy")
    x, z = gx // NZR, gx % NZR
    y, core = gy // 2, gy % 2
    plane = x * 4 + y

    def near_id(dx, dy):
        return ((gx + dx + 64) % 64, (gy + dy + 8) % 8)

    def plane_at(o):
        return ((x + o[0]) % 4) * 4 + (y + o[1]) % 4

    def plane_id(o):
        return (((x + o[0]) % 4) * NZR + z, ((y + o[1]) % 4) * 2 + core)

    def z_id(k):
        return (x * NZR + (z + k) % NZR, gy)

    sibling = (gx, y * 2 + (1 - core))
    barrier = pltpu.get_barrier_semaphore()
    partners = [near_id(dx, dy) for dx, dy in NEAR] + [plane_id(o) for o in AROUND] + [z_id(k) for k in ALONG if min(k, NZR - k) <= 4] + [sibling]
    for partner in partners:
        pl.semaphore_signal(barrier, inc=1, device_id=partner, device_id_type=MESH)
    loads = []
    for i in range(3):
        loads.append(pltpu.make_async_copy(basis_hbm.at[pl.ds(256 * i, 256)], basis_ref.at[pl.ds(256 * i, 256)], load_s.at[4 + i]))
    loads.append(pltpu.make_async_copy(taps_hbm, taps_ref, load_s.at[0]))
    for i in range(3):
        loads.append(pltpu.make_async_copy(snap_hbm.at[pl.ds(128 * i, 128)], snap_ref.at[pl.ds(128 * i, 128)], load_s.at[1 + i]))
    for c in loads:
        c.start()

    sub = lax.broadcasted_iota(jnp.int32, (8, B), 0)
    lane = lax.broadcasted_iota(jnp.int32, (8, B), 1)
    for c in loads[:3]:
        c.wait()
    at = 0
    for b in range(4):
        part = lax.dot_general(basis_ref[:, b * B:(b + 1) * B], basis_ref[:, b * B:512], (((0,), (0,)), ((), ())), preferred_element_type=F32)
        for c in range(4 - b):
            acc[at:at + B, :] = part[:, c * B:(c + 1) * B]
            at += B
    pl.semaphore_wait(barrier, len(partners))
    for k in (4, NZR - 4):
        pl.semaphore_signal(far, inc=1, device_id=z_id(k), device_id_type=MESH)

    def copy(src, dst, ssem, rsem, device):
        c = pltpu.make_async_remote_copy(src_ref=src, dst_ref=dst, send_sem=ssem, recv_sem=rsem, device_id=device, device_id_type=MESH)
        c.start()
        return c

    half = NPLANE * CG
    ca = copy(acc.at[pl.ds((1 - core) * half, half)], recv_a, sa, ra, sibling)
    loads[3].wait()
    taps = taps_ref[...].astype(F32)
    ahead, behind, last = tap_tiles(taps, 2, sub)
    for m in range(0, 128, 2):
        pair = []
        for t in (m, m + 1):
            tile = jnp.where(lane == t, ahead, 0.0)
            tile = jnp.where(lane == (t + 1) % 128, behind, tile)
            pair.append(jnp.where(lane == (t + 127) % 128, last, tile))
        band_ref[8 * m:8 * m + 16, :] = jnp.concatenate(pair, axis=0).astype(BF16)
    for c in loads[4:]:
        c.wait()
    along_z = jnp.dot(snap_ref[...], band_ref[...], preferred_element_type=F32)
    ahead, behind, last = tap_tiles(taps, 0, sub)
    w_ahead = [row_splat(ahead, s) for s in range(8)]
    w_behind = [row_splat(behind, s) for s in range(8)]
    w_last = row_splat(last, 0)
    ahead, behind, last = tap_tiles(taps, 1, sub)
    sums = {}
    for dx in (0, 1, -1):
        for dy in (0, 1, -1):
            sums[dx, dy] = jnp.zeros((8, B), F32)
    for c in range(3):
        cell = [[along_z[(c * 8 + i) * 16 + 8 * h:(c * 8 + i) * 16 + 8 * h + 8, :] for i in range(8)] for h in range(2)]
        for dx in (0, 1, -1):
            part = []
            for h in range(2):
                if dx == -1:
                    part.append(w_last * cell[h][0])
                else:
                    w = w_ahead if dx == 0 else w_behind
                    v = w[0] * cell[h][0]
                    for i in range(1, 8):
                        v = v + w[i] * cell[h][i]
                    part.append(v)
            def put(dy, q, tile):
                total = jnp.sum(tile, axis=0, keepdims=True)
                sums[dx, dy] = jnp.where(sub == 2 * c + q, jnp.broadcast_to(total, (8, B)), sums[dx, dy])
            put(0, 0, ahead * part[0] + last * part[1])
            put(0, 1, behind * part[0] + ahead * part[1])
            put(1, 0, behind * part[1])
            put(-1, 1, last * part[0])
    for e, (dx, dy) in enumerate(NEAR):
        tile = sums[dx, dy]
        if dy == 1:
            tile = jnp.where(gy == 7, 0.0, tile)
        if dy == -1:
            tile = jnp.where(gy == 0, 0.0, tile)
        near_out[e] = tile
    near = [copy(near_out.at[e], near_in.at[e], near_s.at[e], near_r.at[e], near_id(dx, dy)) for e, (dx, dy) in enumerate(NEAR)]
    ca.wait_recv()
    def halved(p):
        rows = pl.ds(p * CG, CG)
        recv_a[rows, :] = recv_a[rows, :] + acc[pl.ds(core * half + p * CG, CG), :]
    cb = []
    for e, o in enumerate(AROUND):
        p = plane_at(o)
        halved(p)
        cb.append(copy(recv_a.at[pl.ds(p * CG, CG)], recv_b.at[e], sb.at[e], rb.at[e], plane_id(o)))
    halved(plane)
    total = recv_a[pl.ds(plane * CG, CG), :]
    for e in reversed(range(NPLANE - 1)):
        cb[e].wait_recv()
        total = total + recv_b[e]
    pl.semaphore_wait(far, 2)
    total = jnp.concatenate([total, jnp.zeros((CH - CG, B), F32)], axis=0)
    for i in range(NZR):
        chunk_ref[i] = total[i * PIECE:(i + 1) * PIECE, :]
    cc = []
    for e, k in enumerate(ALONG):
        cc.append(copy(chunk_ref.at[(z + k) % NZR], recv_c.at[e], sc.at[e], rc.at[e], z_id(k)))
    for c in near:
        c.wait_recv()
    f = sums[0, 0]
    for e in range(len(NEAR)):
        f = f + near_in[e]
    f16 = f.astype(BF16)
    f = f16.astype(F32)
    filt_ref[...] = f[0:6, :]
    frow = jnp.concatenate([jnp.broadcast_to(f[i:i + 1, :], (8, B)) for i in range(6)], axis=1).astype(BF16)
    g = jnp.dot(frow, basis_ref[...], preferred_element_type=F32)
    sq = jnp.where(sub < 6, f * f, 0.0)
    ff = jnp.sum(jnp.sum(sq, axis=1, keepdims=True), axis=0, keepdims=True)
    tail = jnp.where(sub == 4, jnp.broadcast_to(ff, (8, B)), 0.0)
    for i in range(4):
        tail = jnp.where(sub == i, g[:, i * B:(i + 1) * B], tail)
    gsend[...] = tail
    cga = copy(gsend, gsib, sga, rga, sibling)
    cga.wait_recv()
    gin[plane] = tail + gsib[...]
    cgb = [copy(gin.at[plane], gin.at[plane], sgb.at[e], rgb.at[e], plane_id(o)) for e, o in enumerate(AROUND)]
    total = chunk_ref[z]
    for e in reversed(range(NZR - 1)):
        cc[e].wait_recv()
        total = total + recv_c[e]
    piece_ref[...] = total
    cd = []
    for e, k in enumerate(ALONG):
        cd.append(copy(piece_ref, ring_ref.at[z], sd.at[e], rd.at[e], z_id(k)))
    ring_ref[z] = total
    for c in reversed(cgb):
        c.wait_recv()
    column = gin[0]
    for i in range(1, NPLANE):
        column = column + gin[i]
    gout[...] = column
    gz[z] = column
    cgc = [copy(gout, gz.at[z], sgc.at[e], rgc.at[e], z_id(k)) for e, k in enumerate(ALONG)]
    for c in reversed(cd):
        c.wait_recv()
    for i in range(NZR):
        whole_ref[i * PIECE:(i + 1) * PIECE, :] = ring_ref[i]
    rows = pl.ds(0, CG)
    def slot(c, p):
        return full_ref.at[c * NPLANE + p, rows]
    ce = []
    for e, o in enumerate(AROUND):
        ce.append(copy(whole_ref.at[rows], slot(core, plane), se.at[e], re.at[e], plane_id(o)))
    cf = [copy(whole_ref.at[rows], slot(core, plane), sf.at[NPLANE - 1], rf.at[NPLANE - 1], sibling)]
    full_ref[core * NPLANE + plane] = whole_ref[0:CG, :]
    for e in reversed(range(NPLANE - 1)):
        ce[e].wait_recv()
        p = plane_at((4 - AROUND[e][0], 4 - AROUND[e][1]))
        cf.append(copy(slot(core, p), slot(core, p), sf.at[e], rf.at[e], sibling))
    for c in reversed(cgc):
        c.wait_recv()
    column = gz[0]
    for i in range(1, NZR):
        column = column + gz[i]
    col_ref[...] = column
    for c in cf:
        c.wait_recv()
    for c in near + [ca, cga] + cb + cgb + cc + cd + cgc + ce + cf:
        c.wait_send()


def reduced(taps, snap, basis):
    dma = pltpu.SemaphoreType.DMA
    vmem = pltpu.VMEM
    n = NPLANE - 1
    return pl.pallas_call(
        reduce_kernel,
        out_shape=(jax.ShapeDtypeStruct((2 * NPLANE, CG, B), F32), jax.ShapeDtypeStruct((8, B), F32), jax.ShapeDtypeStruct((6, B), F32)),
        in_specs=[pl.BlockSpec(memory_space=pltpu.HBM)] * 3,
        out_specs=[pl.BlockSpec(memory_space=vmem)] * 3,
        scratch_shapes=[
            vmem((3, 17), BF16),
            vmem((384, 1024), BF16),
            vmem((768, 512), BF16),
            vmem((1024, B), BF16),
            vmem((8, 8, B), F32),
            vmem((8, 8, B), F32),
            vmem((2 * NPLANE * CG, B), F32),
            vmem((NPLANE * CG, B), F32),
            vmem((n, CG, B), F32),
            vmem((NZR, PIECE, B), F32),
            vmem((n, PIECE, B), F32),
            vmem((PIECE, B), F32),
            vmem((NZR, PIECE, B), F32),
            vmem((CH, B), F32),
            vmem((8, B), F32),
            vmem((8, B), F32),
            vmem((8, B), F32),
            vmem((NPLANE, 8, B), F32),
            vmem((8, B), F32),
            vmem((NZR, 8, B), F32),
            dma((7,)), dma((8,)), dma((8,)), dma, dma,
            dma((n,)), dma((n,)), dma((n,)), dma((n,)), dma((n,)), dma((n,)), dma((n,)), dma((n,)), dma((n + 1,)), dma((n + 1,)),
            dma, dma, dma((n,)), dma((n,)), dma((n,)), dma((n,)), pltpu.SemaphoreType.REGULAR,
        ],
        compiler_params=pltpu.CompilerParams(vmem_limit_bytes=40<<20, collective_id=0, has_side_effects=True),
        name="reduce",
    )(*(pltpu.with_memory_space_constraint(v, pltpu.HBM) for v in (taps, snap, basis)))


def local(snapshot, basis, taps):
    flat = basis.reshape(-1, basis.shape[-1])
    g, col, f = reduced(taps, snapshot.reshape(-1, snapshot.shape[-1]), flat)
    total = flat.shape[0] * lax.axis_size("gx") * lax.axis_size("gy")
    modes, mode, fac = k2(g, col, f, flat, float(total))
    return modes.reshape(basis.shape), mode.reshape(basis.shape[:-1]), fac


def solution(mesh):
    in_specs = (P(None, "gx", "gy", None), P(None, "gx", "gy", None, None), P())
    out_specs = (P(None, "gx", "gy", None, None), P(None, "gx", "gy", None), P())
    return jax.shard_map(local, mesh=mesh, in_specs=in_specs, out_specs=out_specs, check_vma=False)
```

```python
import functools
import jax, jax.numpy as jnp
from jax import lax
from jax.sharding import PartitionSpec as P
from jax.experimental import pallas as pl
from jax.experimental.pallas import tpu as pltpu

F32, BF16 = jnp.float32, jnp.bfloat16
B, H = 128, 64
HI = lax.Precision.HIGHEST


def lane_splat(tile, lane):
    return jnp.take_along_axis(tile, jnp.full((8, B), lane, jnp.int32), axis=1)


def row_splat(tile, row):
    return jnp.broadcast_to(tile[row:row + 1, :], (8, B))


def nn(x, y):
    return lax.dot_general(x, y, (((1,), (0,)), ((), ())), precision=HI, preferred_element_type=F32)


def tn(x, y):
    return lax.dot_general(x, y, (((0,), (0,)), ((), ())), precision=HI, preferred_element_type=F32)


def nt(x, y):
    return lax.dot_general(x, y, (((1,), (1,)), ((), ())), precision=HI, preferred_element_type=F32)


def nt16(x, y):
    return lax.dot_general(x, y, (((1,), (1,)), ((), ())), preferred_element_type=F32)


def split(x):
    hi = x.astype(BF16)
    return hi, (x - hi.astype(F32)).astype(BF16)


def factor_half(a, off, tick):
    sub = lax.broadcasted_iota(jnp.int32, (8, B), 0)
    lane = lax.broadcasted_iota(jnp.int32, (8, B), 1)
    mine = (lane >= H) if off else (lane < H)
    n = H // 8
    a = [jnp.where(mine, a[t], jnp.where(lane + off - H == 8 * t + sub, 1.0, 0.0)) for t in range(n)]
    diag = [lane_splat(a[0], off + j) for j in range(8)]
    for p in range(n):
        cols = diag
        below = range(p + 1, n)
        c = {t: [lane_splat(a[t], off + 8 * p + j) for j in range(8)] for t in below}
        if below:
            diag = [lane_splat(a[p + 1], off + 8 * (p + 1) + j) for j in range(8)]
        inv, row, mult = [], {}, {}
        pivots = jnp.ones((8, B), F32)
        pivot = row_splat(cols[0], 0)
        for k in range(8):
            pivots = jnp.where(sub == k, pivot, pivots)
            r = pl.reciprocal(pivot, approx=True)
            inv.append(r)
            m = cols[k] * r
            for j in range(k + 1, 8):
                row[k, j] = row_splat(cols[j], k)
            if k < 7:
                pivot = row_splat(cols[k + 1], k + 1) - (row[k, k + 1] * row[k, k + 1]) * r
                for j in range(k + 1, 8):
                    cols[j] = cols[j] - m * row[k, j]
                a[p] = a[p] - jnp.where(sub > k, m, 0.0) * row_splat(a[p], k)
        for t in below:
            for k in range(8):
                mult[t, k] = c[t][k] * inv[k]
                for j in range(k + 1, 8):
                    c[t][j] = c[t][j] - mult[t, k] * row[k, j]
        if below:
            for j in range(8):
                for k in range(8):
                    diag[j] = diag[j] - mult[p + 1, k] * row_splat(c[p + 1][k], j)
            for k in range(8):
                u = row_splat(a[p], k)
                for t in below:
                    a[t] = a[t] - mult[t, k] * u
        a[p] = a[p] * lax.rsqrt(pivots)
        tick()
    return jnp.concatenate(a, axis=0)


def factor_block(x, tick):
    lane = lax.broadcasted_iota(jnp.int32, (H, B), 1)
    rows = lax.broadcasted_iota(jnp.int32, (H, B), 0)
    low = lane < H
    zero = jnp.zeros((H, B), F32)
    p0 = factor_half([x[8 * t:8 * t + 8] for t in range(8)], 0, tick)
    r01 = nn(p0, jnp.concatenate([zero, jnp.where(low, 0.0, x[0:H])], axis=0))
    s11 = x[H:B] - tn(r01, r01)[H:B]
    w0 = jnp.where(low, pltpu.roll(p0, H, 1), 0.0)
    t10 = tn(r01, w0)[H:B]
    p1 = factor_half([s11[8 * t:8 * t + 8] for t in range(8)], H, tick)
    w10 = nn(p1, jnp.concatenate([t10, zero], axis=0))
    r = jnp.concatenate([jnp.where(low, jnp.where(lane >= rows, p0, 0.0), r01), jnp.where(lane >= rows + H, p1, 0.0)], axis=0)
    w = jnp.concatenate([w0, jnp.where(low, -w10, pltpu.roll(p1, H, 1))], axis=0)
    return r, w


PAIRS = [(b, c) for b in range(4) for c in range(b, 4)]
INDEX = {pair: i for i, pair in enumerate(PAIRS)}


def k2_kernel(total, g_ref, col_ref, f_ref, basis_hbm, modes_hbm, mode_ref, factor_hbm, s_ref, zw_ref, zh_ref, zl_ref, basis_ref, modes_ref, factor_ref, load_s, out_s, fac_s):
    load = pltpu.make_async_copy(basis_hbm, basis_ref, load_s)
    load.start()
    scale = 1.0 / total
    for i in range(160):
        s_ref[i // 16, 8 * (i % 16):8 * (i % 16) + 8, :] = g_ref[i // 5, 8 * (i % 5):8 * (i % 5) + 8, :] * scale
    col = col_ref[...] * scale
    g8 = jnp.broadcast_to(jnp.concatenate([col[i:i + 1, :] for i in range(4)], axis=1), (8, 512))
    factor_ref[...] = jnp.zeros_like(factor_ref)
    zw_ref[...] = jnp.zeros_like(zw_ref)
    zh_ref[...] = jnp.zeros_like(zh_ref)
    zl_ref[...] = jnp.zeros_like(zl_ref)
    outs = []
    later = []
    state = [jnp.zeros((8, 512), F32), jnp.zeros((8, 1), F32)]

    def tick():
        if later:
            later.pop(0)()

    def start(src, dst, sem):
        outs.append(pltpu.make_async_copy(src, dst, sem))
        outs[-1].start()

    def panel(b, c):
        return factor_ref[b * B:(b + 1) * B, c * B:(c + 1) * B]

    def factor_off(b, c, w):
        factor_ref[b * B:(b + 1) * B, c * B:(c + 1) * B] = nn(w, s_ref[INDEX[b, c]])

    def inverse_row(b, w):
        lo, hi = b * B, (b + 1) * B
        if b:
            zw_ref[lo:hi, 0:lo] = nn(w, zw_ref[lo:hi, 0:lo])
        zw_ref[lo:hi, lo:hi] = w
        zh_ref[lo:hi, 0:hi], zl_ref[lo:hi, 0:hi] = split(zw_ref[lo:hi, 0:hi])

    def trail(b, i, c):
        s_ref[INDEX[i, c]] = s_ref[INDEX[i, c]] - tn(panel(b, i), panel(b, c))

    def inverse_trail(b, i):
        hi = (b + 1) * B
        zw_ref[i * B:(i + 1) * B, 0:hi] = zw_ref[i * B:(i + 1) * B, 0:hi] - tn(panel(b, i), zw_ref[b * B:hi, 0:hi])

    def column(b):
        lo, hi = b * B, (b + 1) * B
        zrow = zw_ref[lo:hi, :]
        factor_ref[lo:hi, 512:513] = nt(zrow, g8)[:, 0:1]
        start(factor_ref.at[pl.ds(lo, B)], factor_hbm.at[pl.ds(lo, B)], fac_s.at[b])
        rrow = nt(g8, zrow)
        state[1] = state[1] + jnp.sum(rrow * rrow, axis=1, keepdims=True)
        state[0] = state[0] + nn(rrow, zrow)

    def apply(b, part):
        lo, hi = b * B, (b + 1) * B
        if b == 0 and part == 0:
            load.wait()
        top = part * (rows // 2)
        own = basis_ref[top:top + rows // 2, 0:hi]
        out = nt16(own, zh_ref[lo:hi, 0:hi]) + nt16(own, zl_ref[lo:hi, 0:hi])
        modes_ref[top:top + rows // 2, lo:hi] = out.astype(BF16)
        at = (pl.ds(top, rows // 2), pl.ds(lo, B))
        start(modes_ref.at[at], modes_hbm.at[at], out_s.at[2 * b + part])

    rows = basis_ref.shape[0]
    for b in range(4):
        lo, hi = b * B, (b + 1) * B
        r_own, w = factor_block(s_ref[INDEX[b, b]], tick)
        while later:
            tick()
        if b < 3:
            factor_off(b, b + 1, w)
            trail(b, b + 1, b + 1)
        factor_ref[lo:hi, lo:hi] = r_own
        for c in range(b + 2, 4):
            later.append(functools.partial(factor_off, b, c, w))
        later.append(functools.partial(inverse_row, b, w))
        for i in range(b + 1, 4):
            for c in range(i, 4):
                if (i, c) != (b + 1, b + 1):
                    later.append(functools.partial(trail, b, i, c))
            later.append(functools.partial(inverse_trail, b, i))
        if b < 3:
            later.append(functools.partial(column, b))
        later.append(functools.partial(apply, b, 0))
        later.append(functools.partial(apply, b, 1))
        if b == 3:
            later.append(functools.partial(column, b))
    while later:
        tick()
    v, norm = state
    d2 = col[4:5, 0:1] - norm[0:1]
    inv_d = lax.rsqrt(d2)
    factor_ref[512:513, 512:513] = d2 * inv_d
    outs.append(pltpu.make_async_copy(factor_ref.at[pl.ds(512, 1)], factor_hbm.at[pl.ds(512, 1)], fac_s.at[4]))
    outs[-1].start()
    vh, vl = split(v)
    y = nt16(vh, basis_ref[...]) + nt16(vl, basis_ref[...])
    f = f_ref[...]
    for i in range(6):
        mode_ref[i // 2, i % 2:i % 2 + 1, :] = (f[i:i + 1, :] - y[0:1, i * B:(i + 1) * B]) * inv_d
    for c in outs:
        c.wait()


def k2(g, col, f, basis, total):
    rows = basis.shape[0]
    vmem, hbm, dma = pltpu.VMEM, pltpu.HBM, pltpu.SemaphoreType.DMA
    return pl.pallas_call(
        functools.partial(k2_kernel, total),
        out_shape=(jax.ShapeDtypeStruct((rows, 512), BF16), jax.ShapeDtypeStruct((3, 2, B), F32), jax.ShapeDtypeStruct((513, 513), F32)),
        in_specs=[pl.BlockSpec(memory_space=vmem)] * 3 + [pl.BlockSpec(memory_space=hbm)],
        out_specs=[pl.BlockSpec(memory_space=hbm), pl.BlockSpec(memory_space=vmem), pl.BlockSpec(memory_space=hbm)],
        scratch_shapes=[
            vmem((10, B, B), F32), vmem((512, 512), F32), vmem((512, 512), BF16), vmem((512, 512), BF16),
            vmem((rows, 512), BF16), vmem((rows, 512), BF16), vmem((513, 513), F32), dma, dma((8,)), dma((5,)),
        ],
        compiler_params=pltpu.CompilerParams(vmem_limit_bytes=40 << 20),
        name="factor",
    )(g, col, f, basis)

MESH = pl.DeviceIdType.MESH
NPLANE, NZR, CH, CG = 16, 16, 48, 40
PIECE = CH // NZR
NEAR = [(dx, dy) for dx in (0, 1, -1) for dy in (0, 1, -1) if (dx, dy) != (0, 0)]
AROUND = sorted(((dx, dy) for dx in range(4) for dy in range(4) if dx or dy), key=lambda o: -(min(o[0], 4 - o[0]) + min(o[1], 4 - o[1])))
ALONG = sorted(range(1, NZR), key=lambda k: -min(k, NZR - k))


def tap_tiles(taps, d, sub):
    def at(i):
        return jnp.broadcast_to(taps[d:d + 1, i:i + 1], (8, B))
    ahead = behind = jnp.zeros((8, B), F32)
    for s in range(8):
        ahead = jnp.where(sub == s, at(8 + s), ahead)
        behind = jnp.where(sub == s, at(s), behind)
    return ahead, behind, jnp.where(sub == 0, at(16), 0.0)


def reduce_kernel(taps_hbm, snap_hbm, basis_hbm, full_ref, col_ref, filt_ref, taps_ref, snap_ref, basis_ref, band_ref, near_out, near_in, acc, recv_a, recv_b, chunk_ref, recv_c, piece_ref, ring_ref, whole_ref, gsend, grecv, gsib, gin, gout, gz, load_s, near_s, near_r, sa, ra, sb, rb, sc, rc, sd, rd, se, re, sf, rf, sga, rga, sgb, rgb, sgc, rgc, far):
    gx, gy = lax.axis_index("gx"), lax.axis_index("gy")
    x, z = gx // NZR, gx % NZR
    y, core = gy // 2, gy % 2
    plane = x * 4 + y

    def near_id(dx, dy):
        return ((gx + dx + 64) % 64, (gy + dy + 8) % 8)

    def plane_at(o):
        return ((x + o[0]) % 4) * 4 + (y + o[1]) % 4

    def plane_id(o):
        return (((x + o[0]) % 4) * NZR + z, ((y + o[1]) % 4) * 2 + core)

    def z_id(k):
        return (x * NZR + (z + k) % NZR, gy)

    sibling = (gx, y * 2 + (1 - core))
    barrier = pltpu.get_barrier_semaphore()
    partners = [near_id(dx, dy) for dx, dy in NEAR] + [plane_id(o) for o in AROUND] + [z_id(k) for k in ALONG if min(k, NZR - k) <= 4] + [sibling]
    for partner in partners:
        pl.semaphore_signal(barrier, inc=1, device_id=partner, device_id_type=MESH)
    loads = []
    for i in range(3):
        loads.append(pltpu.make_async_copy(basis_hbm.at[pl.ds(256 * i, 256)], basis_ref.at[pl.ds(256 * i, 256)], load_s.at[4 + i]))
    loads.append(pltpu.make_async_copy(taps_hbm, taps_ref, load_s.at[0]))
    for i in range(3):
        loads.append(pltpu.make_async_copy(snap_hbm.at[pl.ds(128 * i, 128)], snap_ref.at[pl.ds(128 * i, 128)], load_s.at[1 + i]))
    for c in loads:
        c.start()

    sub = lax.broadcasted_iota(jnp.int32, (8, B), 0)
    lane = lax.broadcasted_iota(jnp.int32, (8, B), 1)
    for c in loads[:3]:
        c.wait()
    at = 0
    for b in range(4):
        part = lax.dot_general(basis_ref[:, b * B:(b + 1) * B], basis_ref[:, b * B:512], (((0,), (0,)), ((), ())), preferred_element_type=F32)
        for c in range(4 - b):
            acc[at:at + B, :] = part[:, c * B:(c + 1) * B]
            at += B
    pl.semaphore_wait(barrier, len(partners))
    for k in (4, NZR - 4):
        pl.semaphore_signal(far, inc=1, device_id=z_id(k), device_id_type=MESH)

    def copy(src, dst, ssem, rsem, device):
        c = pltpu.make_async_remote_copy(src_ref=src, dst_ref=dst, send_sem=ssem, recv_sem=rsem, device_id=device, device_id_type=MESH)
        c.start()
        return c

    half = NPLANE * CG
    ca = copy(acc.at[pl.ds((1 - core) * half, half)], recv_a, sa, ra, sibling)
    loads[3].wait()
    taps = taps_ref[...].astype(F32)
    ahead, behind, last = tap_tiles(taps, 2, sub)
    for m in range(0, 128, 2):
        pair = []
        for t in (m, m + 1):
            tile = jnp.where(lane == t, ahead, 0.0)
            tile = jnp.where(lane == (t + 1) % 128, behind, tile)
            pair.append(jnp.where(lane == (t + 127) % 128, last, tile))
        band_ref[8 * m:8 * m + 16, :] = jnp.concatenate(pair, axis=0).astype(BF16)
    for c in loads[4:]:
        c.wait()
    along_z = jnp.dot(snap_ref[...], band_ref[...], preferred_element_type=F32)
    ahead, behind, last = tap_tiles(taps, 0, sub)
    w_ahead = [row_splat(ahead, s) for s in range(8)]
    w_behind = [row_splat(behind, s) for s in range(8)]
    w_last = row_splat(last, 0)
    ahead, behind, last = tap_tiles(taps, 1, sub)
    sums = {}
    for dx in (0, 1, -1):
        for dy in (0, 1, -1):
            sums[dx, dy] = jnp.zeros((8, B), F32)
    for c in range(3):
        cell = [[along_z[(c * 8 + i) * 16 + 8 * h:(c * 8 + i) * 16 + 8 * h + 8, :] for i in range(8)] for h in range(2)]
        for dx in (0, 1, -1):
            part = []
            for h in range(2):
                if dx == -1:
                    part.append(w_last * cell[h][0])
                else:
                    w = w_ahead if dx == 0 else w_behind
                    v = w[0] * cell[h][0]
                    for i in range(1, 8):
                        v = v + w[i] * cell[h][i]
                    part.append(v)
            def put(dy, q, tile):
                total = jnp.sum(tile, axis=0, keepdims=True)
                sums[dx, dy] = jnp.where(sub == 2 * c + q, jnp.broadcast_to(total, (8, B)), sums[dx, dy])
            put(0, 0, ahead * part[0] + last * part[1])
            put(0, 1, behind * part[0] + ahead * part[1])
            put(1, 0, behind * part[1])
            put(-1, 1, last * part[0])
    for e, (dx, dy) in enumerate(NEAR):
        tile = sums[dx, dy]
        if dy == 1:
            tile = jnp.where(gy == 7, 0.0, tile)
        if dy == -1:
            tile = jnp.where(gy == 0, 0.0, tile)
        near_out[e] = tile
    near = [copy(near_out.at[e], near_in.at[e], near_s.at[e], near_r.at[e], near_id(dx, dy)) for e, (dx, dy) in enumerate(NEAR)]
    ca.wait_recv()
    def halved(p):
        rows = pl.ds(p * CG, CG)
        recv_a[rows, :] = recv_a[rows, :] + acc[pl.ds(core * half + p * CG, CG), :]
    cb = []
    for e, o in enumerate(AROUND):
        p = plane_at(o)
        halved(p)
        cb.append(copy(recv_a.at[pl.ds(p * CG, CG)], recv_b.at[e], sb.at[e], rb.at[e], plane_id(o)))
    halved(plane)
    total = recv_a[pl.ds(plane * CG, CG), :]
    for e in reversed(range(NPLANE - 1)):
        cb[e].wait_recv()
        total = total + recv_b[e]
    pl.semaphore_wait(far, 2)
    total = jnp.concatenate([total, jnp.zeros((CH - CG, B), F32)], axis=0)
    for i in range(NZR):
        chunk_ref[i] = total[i * PIECE:(i + 1) * PIECE, :]
    cc = []
    for e, k in enumerate(ALONG):
        cc.append(copy(chunk_ref.at[(z + k) % NZR], recv_c.at[e], sc.at[e], rc.at[e], z_id(k)))
    for c in near:
        c.wait_recv()
    f = sums[0, 0]
    for e in range(len(NEAR)):
        f = f + near_in[e]
    f16 = f.astype(BF16)
    f = f16.astype(F32)
    filt_ref[...] = f[0:6, :]
    frow = jnp.concatenate([jnp.broadcast_to(f[i:i + 1, :], (8, B)) for i in range(6)], axis=1).astype(BF16)
    g = jnp.dot(frow, basis_ref[...], preferred_element_type=F32)
    sq = jnp.where(sub < 6, f * f, 0.0)
    ff = jnp.sum(jnp.sum(sq, axis=1, keepdims=True), axis=0, keepdims=True)
    tail = jnp.where(sub == 4, jnp.broadcast_to(ff, (8, B)), 0.0)
    for i in range(4):
        tail = jnp.where(sub == i, g[:, i * B:(i + 1) * B], tail)
    gsend[...] = tail
    cga = copy(gsend, gsib, sga, rga, sibling)
    cga.wait_recv()
    gin[plane] = tail + gsib[...]
    cgb = [copy(gin.at[plane], gin.at[plane], sgb.at[e], rgb.at[e], plane_id(o)) for e, o in enumerate(AROUND)]
    total = chunk_ref[z]
    for e in reversed(range(NZR - 1)):
        cc[e].wait_recv()
        total = total + recv_c[e]
    piece_ref[...] = total
    cd = []
    for e, k in enumerate(ALONG):
        cd.append(copy(piece_ref, ring_ref.at[z], sd.at[e], rd.at[e], z_id(k)))
    ring_ref[z] = total
    for c in reversed(cgb):
        c.wait_recv()
    column = gin[0]
    for i in range(1, NPLANE):
        column = column + gin[i]
    gout[...] = column
    gz[z] = column
    cgc = [copy(gout, gz.at[z], sgc.at[e], rgc.at[e], z_id(k)) for e, k in enumerate(ALONG)]
    for c in reversed(cd):
        c.wait_recv()
    for i in range(NZR):
        whole_ref[i * PIECE:(i + 1) * PIECE, :] = ring_ref[i]
    rows = pl.ds(0, CG)
    def slot(c, p):
        return full_ref.at[c * NPLANE + p, rows]
    ce = []
    for e, o in enumerate(AROUND):
        ce.append(copy(whole_ref.at[rows], slot(core, plane), se.at[e], re.at[e], plane_id(o)))
    cf = [copy(whole_ref.at[rows], slot(core, plane), sf.at[NPLANE - 1], rf.at[NPLANE - 1], sibling)]
    full_ref[core * NPLANE + plane] = whole_ref[0:CG, :]
    for e in reversed(range(NPLANE - 1)):
        ce[e].wait_recv()
        p = plane_at((4 - AROUND[e][0], 4 - AROUND[e][1]))
        cf.append(copy(slot(core, p), slot(core, p), sf.at[e], rf.at[e], sibling))
    for c in reversed(cgc):
        c.wait_recv()
    column = gz[0]
    for i in range(1, NZR):
        column = column + gz[i]
    col_ref[...] = column
    for c in cf:
        c.wait_recv()
    for c in near + [ca, cga] + cb + cgb + cc + cd + cgc + ce + cf:
        c.wait_send()


def reduced(taps, snap, basis):
    dma = pltpu.SemaphoreType.DMA
    vmem = pltpu.VMEM
    n = NPLANE - 1
    return pl.pallas_call(
        reduce_kernel,
        out_shape=(jax.ShapeDtypeStruct((2 * NPLANE, CG, B), F32), jax.ShapeDtypeStruct((8, B), F32), jax.ShapeDtypeStruct((6, B), F32)),
        in_specs=[pl.BlockSpec(memory_space=pltpu.HBM)] * 3,
        out_specs=[pl.BlockSpec(memory_space=vmem)] * 3,
        scratch_shapes=[
            vmem((3, 17), BF16),
            vmem((384, 1024), BF16),
            vmem((768, 512), BF16),
            vmem((1024, B), BF16),
            vmem((8, 8, B), F32),
            vmem((8, 8, B), F32),
            vmem((2 * NPLANE * CG, B), F32),
            vmem((NPLANE * CG, B), F32),
            vmem((n, CG, B), F32),
            vmem((NZR, PIECE, B), F32),
            vmem((n, PIECE, B), F32),
            vmem((PIECE, B), F32),
            vmem((NZR, PIECE, B), F32),
            vmem((CH, B), F32),
            vmem((8, B), F32),
            vmem((8, B), F32),
            vmem((8, B), F32),
            vmem((NPLANE, 8, B), F32),
            vmem((8, B), F32),
            vmem((NZR, 8, B), F32),
            dma((7,)), dma((8,)), dma((8,)), dma, dma,
            dma((n,)), dma((n,)), dma((n,)), dma((n,)), dma((n,)), dma((n,)), dma((n,)), dma((n,)), dma((n + 1,)), dma((n + 1,)),
            dma, dma, dma((n,)), dma((n,)), dma((n,)), dma((n,)), pltpu.SemaphoreType.REGULAR,
        ],
        compiler_params=pltpu.CompilerParams(vmem_limit_bytes=40<<20, collective_id=0, has_side_effects=True),
        name="reduce",
    )(*(pltpu.with_memory_space_constraint(v, pltpu.HBM) for v in (taps, snap, basis)))


def local(snapshot, basis, taps):
    flat = basis.reshape(-1, basis.shape[-1])
    g, col, f = reduced(taps, snapshot.reshape(-1, snapshot.shape[-1]), flat)
    total = flat.shape[0] * lax.axis_size("gx") * lax.axis_size("gy")
    modes, mode, fac = k2(g, col, f, flat, float(total))
    return modes.reshape(basis.shape), mode.reshape(basis.shape[:-1]), fac


def solution(mesh):
    in_specs = (P(None, "gx", "gy", None), P(None, "gx", "gy", None, None), P())
    out_specs = (P(None, "gx", "gy", None, None), P(None, "gx", "gy", None), P())
    return jax.shard_map(local, mesh=mesh, in_specs=in_specs, out_specs=out_specs, check_vma=False)
```

```python
import functools
import jax, jax.numpy as jnp
from jax import lax
from jax.sharding import PartitionSpec as P
from jax.experimental import pallas as pl
from jax.experimental.pallas import tpu as pltpu

F32, BF16 = jnp.float32, jnp.bfloat16
B, H = 128, 64
HI = lax.Precision.HIGHEST


def lane_splat(tile, lane):
    return jnp.take_along_axis(tile, jnp.full((8, B), lane, jnp.int32), axis=1)


def row_splat(tile, row):
    return jnp.broadcast_to(tile[row:row + 1, :], (8, B))


def nn(x, y):
    return lax.dot_general(x, y, (((1,), (0,)), ((), ())), precision=HI, preferred_element_type=F32)


def tn(x, y):
    return lax.dot_general(x, y, (((0,), (0,)), ((), ())), precision=HI, preferred_element_type=F32)


def nt(x, y):
    return lax.dot_general(x, y, (((1,), (1,)), ((), ())), precision=HI, preferred_element_type=F32)


def nt16(x, y):
    return lax.dot_general(x, y, (((1,), (1,)), ((), ())), preferred_element_type=F32)


def split(x):
    hi = x.astype(BF16)
    return hi, (x - hi.astype(F32)).astype(BF16)


def factor_half(a, off, tick):
    sub = lax.broadcasted_iota(jnp.int32, (8, B), 0)
    lane = lax.broadcasted_iota(jnp.int32, (8, B), 1)
    mine = (lane >= H) if off else (lane < H)
    n = H // 8
    a = [jnp.where(mine, a[t], jnp.where(lane + off - H == 8 * t + sub, 1.0, 0.0)) for t in range(n)]
    diag = [lane_splat(a[0], off + j) for j in range(8)]
    for p in range(n):
        cols = diag
        below = range(p + 1, n)
        c = {t: [lane_splat(a[t], off + 8 * p + j) for j in range(8)] for t in below}
        if below:
            diag = [lane_splat(a[p + 1], off + 8 * (p + 1) + j) for j in range(8)]
        inv, row, mult = [], {}, {}
        pivots = jnp.ones((8, B), F32)
        pivot = row_splat(cols[0], 0)
        for k in range(8):
            pivots = jnp.where(sub == k, pivot, pivots)
            r = pl.reciprocal(pivot, approx=True)
            inv.append(r)
            m = cols[k] * r
            for j in range(k + 1, 8):
                row[k, j] = row_splat(cols[j], k)
            if k < 7:
                pivot = row_splat(cols[k + 1], k + 1) - (row[k, k + 1] * row[k, k + 1]) * r
                for j in range(k + 1, 8):
                    cols[j] = cols[j] - m * row[k, j]
                a[p] = a[p] - jnp.where(sub > k, m, 0.0) * row_splat(a[p], k)
        for t in below:
            for k in range(8):
                mult[t, k] = c[t][k] * inv[k]
                for j in range(k + 1, 8):
                    c[t][j] = c[t][j] - mult[t, k] * row[k, j]
        if below:
            for j in range(8):
                for k in range(8):
                    diag[j] = diag[j] - mult[p + 1, k] * row_splat(c[p + 1][k], j)
            for k in range(8):
                u = row_splat(a[p], k)
                for t in below:
                    a[t] = a[t] - mult[t, k] * u
        a[p] = a[p] * lax.rsqrt(pivots)
        tick()
    return jnp.concatenate(a, axis=0)


def factor_block(x, tick):
    lane = lax.broadcasted_iota(jnp.int32, (H, B), 1)
    rows = lax.broadcasted_iota(jnp.int32, (H, B), 0)
    low = lane < H
    zero = jnp.zeros((H, B), F32)
    p0 = factor_half([x[8 * t:8 * t + 8] for t in range(8)], 0, tick)
    r01 = nn(p0, jnp.concatenate([zero, jnp.where(low, 0.0, x[0:H])], axis=0))
    s11 = x[H:B] - tn(r01, r01)[H:B]
    w0 = jnp.where(low, pltpu.roll(p0, H, 1), 0.0)
    t10 = tn(r01, w0)[H:B]
    p1 = factor_half([s11[8 * t:8 * t + 8] for t in range(8)], H, tick)
    w10 = nn(p1, jnp.concatenate([t10, zero], axis=0))
    r = jnp.concatenate([jnp.where(low, jnp.where(lane >= rows, p0, 0.0), r01), jnp.where(lane >= rows + H, p1, 0.0)], axis=0)
    w = jnp.concatenate([w0, jnp.where(low, -w10, pltpu.roll(p1, H, 1))], axis=0)
    return r, w


OFF = [(b, c) for b in range(4) for c in range(b + 1, 4)]
PAIRS = [(b, c) for b in range(4) for c in range(b, 4)]
INDEX = {pair: i for i, pair in enumerate(PAIRS)}


def k2_kernel(total, g_ref, col_ref, f_ref, basis_hbm, modes_hbm, mode_ref, factor_hbm, s_ref, zw_ref, zh_ref, zl_ref, basis_ref, modes_ref, factor_ref, v_ref, load_s, out_s, fac_s):
    load = pltpu.make_async_copy(basis_hbm, basis_ref, load_s)
    load.start()
    scale = 1.0 / total
    brow = lax.broadcasted_iota(jnp.int32, (B, B), 0)
    bcol = lax.broadcasted_iota(jnp.int32, (B, B), 1)
    col = col_ref[...] * scale
    g8 = jnp.broadcast_to(jnp.concatenate([col[i:i + 1, :] for i in range(4)], axis=1), (8, 512))

    def stored(i):
        return jnp.concatenate([g_ref[4 * i + j] for j in range(4)], axis=0) * scale

    def unpack(i):
        both = stored(6 + i)
        flip = jnp.transpose(both)
        diag = jnp.broadcast_to(col[5 + i:6 + i, :], (B, B))
        s_ref[INDEX[2 * i + 1, 2 * i + 1]] = jnp.where(brow == bcol, diag, jnp.where(brow > bcol, both, flip))
        return jnp.where(brow <= bcol, both, flip)

    def unpack_last():
        s_ref[INDEX[2, 2]] = unpack(1)

    def keep(i):
        s_ref[INDEX[OFF[i]]] = stored(i)

    def clear(b):
        factor_ref[b * B:(b + 1) * B, 0:b * B] = jnp.zeros((B, b * B), F32)

    factor_ref[512:513, :] = jnp.zeros((1, 513), F32)
    v_ref[...] = jnp.zeros_like(v_ref)
    outs = []
    later = [functools.partial(keep, i) for i in range(6)] + [unpack_last] + [functools.partial(clear, b) for b in range(1, 4)]
    state = [jnp.zeros((8, 1), F32)]

    def tick():
        if later:
            later.pop(0)()

    def start(src, dst, sem):
        outs.append(pltpu.make_async_copy(src, dst, sem))
        outs[-1].start()

    def panel(b, c):
        return factor_ref[b * B:(b + 1) * B, c * B:(c + 1) * B]

    def factor_off(b, c, w):
        factor_ref[b * B:(b + 1) * B, c * B:(c + 1) * B] = nn(w, s_ref[INDEX[b, c]])

    def inverse_row(b, w):
        lo, hi = b * B, (b + 1) * B
        if b:
            zw_ref[lo:hi, 0:lo] = nn(w, zw_ref[lo:hi, 0:lo])
        zw_ref[lo:hi, lo:hi] = w
        zh_ref[lo:hi, 0:hi], zl_ref[lo:hi, 0:hi] = split(zw_ref[lo:hi, 0:hi])

    def trail(b, i, c):
        s_ref[INDEX[i, c]] = s_ref[INDEX[i, c]] - tn(panel(b, i), panel(b, c))

    def inverse_trail(b, i):
        lo, hi = b * B, (b + 1) * B
        part = tn(panel(b, i), zw_ref[lo:hi, 0:hi])
        if b:
            zw_ref[i * B:(i + 1) * B, 0:lo] = zw_ref[i * B:(i + 1) * B, 0:lo] - part[:, 0:lo]
        zw_ref[i * B:(i + 1) * B, lo:hi] = -part[:, lo:hi]

    def column(b):
        lo, hi = b * B, (b + 1) * B
        zrow = zw_ref[lo:hi, 0:hi]
        factor_ref[lo:hi, 512:513] = nt(zrow, g8[:, 0:hi])[:, 0:1]
        start(factor_ref.at[pl.ds(lo, B)], factor_hbm.at[pl.ds(lo, B)], fac_s.at[b])
        rrow = nt(g8[:, 0:hi], zrow)
        state[0] = state[0] + jnp.sum(rrow * rrow, axis=1, keepdims=True)
        v_ref[:, 0:hi] = v_ref[:, 0:hi] + nn(rrow, zrow)

    def apply(b, part):
        lo, hi = b * B, (b + 1) * B
        if b == 0 and part == 0:
            load.wait()
        top = part * (rows // 2)
        own = basis_ref[top:top + rows // 2, 0:hi]
        out = nt16(own, zh_ref[lo:hi, 0:hi]) + nt16(own, zl_ref[lo:hi, 0:hi])
        modes_ref[top:top + rows // 2, lo:hi] = out.astype(BF16)
        at = (pl.ds(top, rows // 2), pl.ds(lo, B))
        start(modes_ref.at[at], modes_hbm.at[at], out_s.at[2 * b + part])

    rows = basis_ref.shape[0]
    for b in range(4):
        lo, hi = b * B, (b + 1) * B
        r_own, w = factor_block(s_ref[INDEX[b, b]] if b else unpack(0), tick)
        while later:
            tick()
        if b < 3:
            factor_off(b, b + 1, w)
            trail(b, b + 1, b + 1)
        factor_ref[lo:hi, lo:hi] = r_own
        for c in range(b + 2, 4):
            later.append(functools.partial(factor_off, b, c, w))
        later.append(functools.partial(inverse_row, b, w))
        for i in range(b + 1, 4):
            for c in range(i, 4):
                if (i, c) != (b + 1, b + 1):
                    later.append(functools.partial(trail, b, i, c))
            later.append(functools.partial(inverse_trail, b, i))
        if b < 3:
            later.append(functools.partial(column, b))
        later.append(functools.partial(apply, b, 0))
        later.append(functools.partial(apply, b, 1))
        if b == 3:
            later.append(functools.partial(column, b))
    while later:
        tick()
    v, norm = v_ref[...], state[0]
    d2 = col[4:5, 0:1] - norm[0:1]
    inv_d = lax.rsqrt(d2)
    factor_ref[512:513, 512:513] = d2 * inv_d
    outs.append(pltpu.make_async_copy(factor_ref.at[pl.ds(512, 1)], factor_hbm.at[pl.ds(512, 1)], fac_s.at[4]))
    outs[-1].start()
    vh, vl = split(v)
    y = nt16(vh, basis_ref[...]) + nt16(vl, basis_ref[...])
    f = f_ref[...]
    for i in range(6):
        mode_ref[i // 2, i % 2:i % 2 + 1, :] = (f[i:i + 1, :] - y[0:1, i * B:(i + 1) * B]) * inv_d
    for c in outs:
        c.wait()


def k2(g, col, f, basis, total):
    rows = basis.shape[0]
    vmem, hbm, dma = pltpu.VMEM, pltpu.HBM, pltpu.SemaphoreType.DMA
    return pl.pallas_call(
        functools.partial(k2_kernel, total),
        out_shape=(jax.ShapeDtypeStruct((rows, 512), BF16), jax.ShapeDtypeStruct((3, 2, B), F32), jax.ShapeDtypeStruct((513, 513), F32)),
        in_specs=[pl.BlockSpec(memory_space=vmem)] * 3 + [pl.BlockSpec(memory_space=hbm)],
        out_specs=[pl.BlockSpec(memory_space=hbm), pl.BlockSpec(memory_space=vmem), pl.BlockSpec(memory_space=hbm)],
        scratch_shapes=[
            vmem((10, B, B), F32), vmem((512, 512), F32), vmem((512, 512), BF16), vmem((512, 512), BF16),
            vmem((rows, 512), BF16), vmem((rows, 512), BF16), vmem((513, 513), F32), vmem((8, 512), F32), dma, dma((8,)), dma((5,)),
        ],
        compiler_params=pltpu.CompilerParams(vmem_limit_bytes=40 << 20),
        name="factor",
    )(g, col, f, basis)

MESH = pl.DeviceIdType.MESH
NPLANE, NZR, CH = 16, 16, 32
PIECE = CH // NZR
NEAR = [(dx, dy) for dx in (0, 1, -1) for dy in (0, 1, -1) if (dx, dy) != (0, 0)]
AROUND = sorted(((dx, dy) for dx in range(4) for dy in range(4) if dx or dy), key=lambda o: -(min(o[0], 4 - o[0]) + min(o[1], 4 - o[1])))
ALONG = sorted(range(1, NZR), key=lambda k: -min(k, NZR - k))


def tap_tiles(taps, d, sub):
    def at(i):
        return jnp.broadcast_to(taps[d:d + 1, i:i + 1], (8, B))
    ahead = behind = jnp.zeros((8, B), F32)
    for s in range(8):
        ahead = jnp.where(sub == s, at(8 + s), ahead)
        behind = jnp.where(sub == s, at(s), behind)
    return ahead, behind, jnp.where(sub == 0, at(16), 0.0)


def reduce_kernel(taps_hbm, snap_hbm, basis_hbm, full_ref, col_ref, filt_ref, taps_ref, snap_ref, basis_ref, band_ref, near_out, near_in, acc, recv_a, recv_b, chunk_ref, recv_c, piece_ref, ring_ref, whole_ref, gsend, grecv, gsib, gin, gout, gz, load_s, near_s, near_r, sa, ra, sb, rb, sc, rc, sd, rd, se, re, sf, rf, sga, rga, sgb, rgb, sgc, rgc, second, third):
    gx, gy = lax.axis_index("gx"), lax.axis_index("gy")
    x, z = gx // NZR, gx % NZR
    y, core = gy // 2, gy % 2
    plane = x * 4 + y

    def near_id(dx, dy):
        return ((gx + dx + 64) % 64, (gy + dy + 8) % 8)

    def plane_at(o):
        return ((x + o[0]) % 4) * 4 + (y + o[1]) % 4

    def plane_id(o):
        return (((x + o[0]) % 4) * NZR + z, ((y + o[1]) % 4) * 2 + core)

    def z_id(k):
        return (x * NZR + (z + k) % NZR, gy)

    sibling = (gx, y * 2 + (1 - core))
    barrier = pltpu.get_barrier_semaphore()
    partners = [sibling] + [plane_id(o) for o in AROUND if 0 in o] + [z_id(k) for k in (1, 2, NZR - 2, NZR - 1)]
    for partner in partners:
        pl.semaphore_signal(barrier, inc=1, device_id=partner, device_id_type=MESH)
    loads = []
    for i in range(3):
        loads.append(pltpu.make_async_copy(basis_hbm.at[pl.ds(256 * i, 256)], basis_ref.at[pl.ds(256 * i, 256)], load_s.at[4 + i]))
    loads.append(pltpu.make_async_copy(taps_hbm, taps_ref, load_s.at[0]))
    for i in range(3):
        loads.append(pltpu.make_async_copy(snap_hbm.at[pl.ds(128 * i, 128)], snap_ref.at[pl.ds(128 * i, 128)], load_s.at[1 + i]))
    for c in loads:
        c.start()

    sub = lax.broadcasted_iota(jnp.int32, (8, B), 0)
    lane = lax.broadcasted_iota(jnp.int32, (8, B), 1)
    for c in loads[:3]:
        c.wait()
    own = {}
    for b in range(4):
        part = lax.dot_general(basis_ref[:, b * B:(b + 1) * B], basis_ref[:, b * B:512], (((0,), (0,)), ((), ())), preferred_element_type=F32)
        for c in range(b, 4):
            if c == b:
                own[b] = part[:, 0:B]
            else:
                at = OFF.index((b, c)) * B
                acc[at:at + B, :] = part[:, (c - b) * B:(c - b + 1) * B]
    brow = lax.broadcasted_iota(jnp.int32, (B, B), 0)
    bcol = lax.broadcasted_iota(jnp.int32, (B, B), 1)
    for i in range(2):
        acc[768 + i * B:896 + i * B, :] = jnp.where(brow <= bcol, own[2 * i], own[2 * i + 1])
    diag = [jnp.sum(jnp.where(brow == bcol, own[i], 0.0), axis=0, keepdims=True) for i in (1, 3)]
    pl.semaphore_wait(barrier, len(partners))
    for partner in partners:
        pl.semaphore_signal(second, inc=1, device_id=partner, device_id_type=MESH)

    def copy(src, dst, ssem, rsem, device):
        c = pltpu.make_async_remote_copy(src_ref=src, dst_ref=dst, send_sem=ssem, recv_sem=rsem, device_id=device, device_id_type=MESH)
        c.start()
        return c

    half = NPLANE * CH
    ca = copy(acc.at[pl.ds((1 - core) * half, half)], recv_a, sa, ra, sibling)
    loads[3].wait()
    taps = taps_ref[...].astype(F32)
    ahead, behind, last = tap_tiles(taps, 2, sub)
    for m in range(0, 128, 2):
        pair = []
        for t in (m, m + 1):
            tile = jnp.where(lane == t, ahead, 0.0)
            tile = jnp.where(lane == (t + 1) % 128, behind, tile)
            pair.append(jnp.where(lane == (t + 127) % 128, last, tile))
        band_ref[8 * m:8 * m + 16, :] = jnp.concatenate(pair, axis=0).astype(BF16)
    for c in loads[4:]:
        c.wait()
    along_z = jnp.dot(snap_ref[...], band_ref[...], preferred_element_type=F32)
    ahead, behind, last = tap_tiles(taps, 0, sub)
    w_ahead = [row_splat(ahead, s) for s in range(8)]
    w_behind = [row_splat(behind, s) for s in range(8)]
    w_last = row_splat(last, 0)
    ahead, behind, last = tap_tiles(taps, 1, sub)
    sums = {}
    for dx in (0, 1, -1):
        for dy in (0, 1, -1):
            sums[dx, dy] = jnp.zeros((8, B), F32)
    for c in range(3):
        cell = [[along_z[(c * 8 + i) * 16 + 8 * h:(c * 8 + i) * 16 + 8 * h + 8, :] for i in range(8)] for h in range(2)]
        for dx in (0, 1, -1):
            part = []
            for h in range(2):
                if dx == -1:
                    part.append(w_last * cell[h][0])
                else:
                    w = w_ahead if dx == 0 else w_behind
                    v = w[0] * cell[h][0]
                    for i in range(1, 8):
                        v = v + w[i] * cell[h][i]
                    part.append(v)
            def put(dy, q, tile):
                total = jnp.sum(tile, axis=0, keepdims=True)
                sums[dx, dy] = jnp.where(sub == 2 * c + q, jnp.broadcast_to(total, (8, B)), sums[dx, dy])
            put(0, 0, ahead * part[0] + last * part[1])
            put(0, 1, behind * part[0] + ahead * part[1])
            put(1, 0, behind * part[1])
            put(-1, 1, last * part[0])
    for e, (dx, dy) in enumerate(NEAR):
        tile = sums[dx, dy]
        if dy == 1:
            tile = jnp.where(gy == 7, 0.0, tile)
        if dy == -1:
            tile = jnp.where(gy == 0, 0.0, tile)
        near_out[e] = tile
    pl.semaphore_wait(second, len(partners))
    third_id = [z_id(4), z_id(NZR - 4), near_id(1, 0), near_id(-1, 0)]
    for partner in third_id:
        pl.semaphore_signal(third, inc=1, device_id=partner, device_id_type=MESH)
    ca.wait_recv()
    def halved(p):
        rows = pl.ds(p * CH, CH)
        recv_a[rows, :] = recv_a[rows, :] + acc[pl.ds(core * half + p * CH, CH), :]
    cb = []
    for e, o in enumerate(AROUND):
        p = plane_at(o)
        halved(p)
        cb.append(copy(recv_a.at[pl.ds(p * CH, CH)], recv_b.at[e], sb.at[e], rb.at[e], plane_id(o)))
    halved(plane)
    pl.semaphore_wait(third, len(third_id))
    near = [copy(near_out.at[e], near_in.at[e], near_s.at[e], near_r.at[e], near_id(dx, dy)) for e, (dx, dy) in enumerate(NEAR)]
    total = recv_a[pl.ds(plane * CH, CH), :]
    for e in reversed(range(NPLANE - 1)):
        cb[e].wait_recv()
        total = total + recv_b[e]
    for i in range(NZR):
        chunk_ref[i] = total[i * PIECE:(i + 1) * PIECE, :]
    cc = []
    for e, k in enumerate(ALONG):
        cc.append(copy(chunk_ref.at[(z + k) % NZR], recv_c.at[e], sc.at[e], rc.at[e], z_id(k)))
    for c in near:
        c.wait_recv()
    f = sums[0, 0]
    for e in range(len(NEAR)):
        f = f + near_in[e]
    f16 = f.astype(BF16)
    f = f16.astype(F32)
    filt_ref[...] = f[0:6, :]
    frow = jnp.concatenate([jnp.broadcast_to(f[i:i + 1, :], (8, B)) for i in range(6)], axis=1).astype(BF16)
    g = jnp.dot(frow, basis_ref[...], preferred_element_type=F32)
    sq = jnp.where(sub < 6, f * f, 0.0)
    ff = jnp.sum(jnp.sum(sq, axis=1, keepdims=True), axis=0, keepdims=True)
    tail = jnp.where(sub == 4, jnp.broadcast_to(ff, (8, B)), 0.0)
    for i in range(2):
        tail = jnp.where(sub == 5 + i, jnp.broadcast_to(diag[i], (8, B)), tail)
    for i in range(4):
        tail = jnp.where(sub == i, g[:, i * B:(i + 1) * B], tail)
    gsend[...] = tail
    cga = copy(gsend, gsib, sga, rga, sibling)
    cga.wait_recv()
    gin[plane] = tail + gsib[...]
    cgb = [copy(gin.at[plane], gin.at[plane], sgb.at[e], rgb.at[e], plane_id(o)) for e, o in enumerate(AROUND)]
    total = chunk_ref[z]
    for e in reversed(range(NZR - 1)):
        cc[e].wait_recv()
        total = total + recv_c[e]
    piece_ref[...] = total
    cd = []
    for e, k in enumerate(ALONG):
        cd.append(copy(piece_ref, ring_ref.at[z], sd.at[e], rd.at[e], z_id(k)))
    ring_ref[z] = total
    for c in reversed(cgb):
        c.wait_recv()
    column = gin[0]
    for i in range(1, NPLANE):
        column = column + gin[i]
    gout[...] = column
    gz[z] = column
    cgc = [copy(gout, gz.at[z], sgc.at[e], rgc.at[e], z_id(k)) for e, k in enumerate(ALONG)]
    for c in reversed(cd):
        c.wait_recv()
    for i in range(NZR):
        whole_ref[i * PIECE:(i + 1) * PIECE, :] = ring_ref[i]
    rows = pl.ds(0, CH)
    def slot(c, p):
        return full_ref.at[c * NPLANE + p, rows]
    ce = []
    for e, o in enumerate(AROUND):
        ce.append(copy(whole_ref.at[rows], slot(core, plane), se.at[e], re.at[e], plane_id(o)))
    cf = [copy(whole_ref.at[rows], slot(core, plane), sf.at[NPLANE - 1], rf.at[NPLANE - 1], sibling)]
    full_ref[core * NPLANE + plane] = whole_ref[...]
    for e in reversed(range(NPLANE - 1)):
        ce[e].wait_recv()
        p = plane_at((4 - AROUND[e][0], 4 - AROUND[e][1]))
        cf.append(copy(slot(core, p), slot(core, p), sf.at[e], rf.at[e], sibling))
    for c in reversed(cgc):
        c.wait_recv()
    column = gz[0]
    for i in range(1, NZR):
        column = column + gz[i]
    col_ref[...] = column
    for c in cf:
        c.wait_recv()
    for c in near + [ca, cga] + cb + cgb + cc + cd + cgc + ce + cf:
        c.wait_send()


def reduced(taps, snap, basis):
    dma = pltpu.SemaphoreType.DMA
    vmem = pltpu.VMEM
    n = NPLANE - 1
    return pl.pallas_call(
        reduce_kernel,
        out_shape=(jax.ShapeDtypeStruct((2 * NPLANE, CH, B), F32), jax.ShapeDtypeStruct((8, B), F32), jax.ShapeDtypeStruct((6, B), F32)),
        in_specs=[pl.BlockSpec(memory_space=pltpu.HBM)] * 3,
        out_specs=[pl.BlockSpec(memory_space=vmem)] * 3,
        scratch_shapes=[
            vmem((3, 17), BF16),
            vmem((384, 1024), BF16),
            vmem((768, 512), BF16),
            vmem((1024, B), BF16),
            vmem((8, 8, B), F32),
            vmem((8, 8, B), F32),
            vmem((2 * NPLANE * CH, B), F32),
            vmem((NPLANE * CH, B), F32),
            vmem((n, CH, B), F32),
            vmem((NZR, PIECE, B), F32),
            vmem((n, PIECE, B), F32),
            vmem((PIECE, B), F32),
            vmem((NZR, PIECE, B), F32),
            vmem((CH, B), F32),
            vmem((8, B), F32),
            vmem((8, B), F32),
            vmem((8, B), F32),
            vmem((NPLANE, 8, B), F32),
            vmem((8, B), F32),
            vmem((NZR, 8, B), F32),
            dma((7,)), dma((8,)), dma((8,)), dma, dma,
            dma((n,)), dma((n,)), dma((n,)), dma((n,)), dma((n,)), dma((n,)), dma((n,)), dma((n,)), dma((n + 1,)), dma((n + 1,)),
            dma, dma, dma((n,)), dma((n,)), dma((n,)), dma((n,)), pltpu.SemaphoreType.REGULAR, pltpu.SemaphoreType.REGULAR,
        ],
        compiler_params=pltpu.CompilerParams(vmem_limit_bytes=40<<20, collective_id=0, has_side_effects=True),
        name="reduce",
    )(*(pltpu.with_memory_space_constraint(v, pltpu.HBM) for v in (taps, snap, basis)))


def local(snapshot, basis, taps):
    flat = basis.reshape(-1, basis.shape[-1])
    g, col, f = reduced(taps, snapshot.reshape(-1, snapshot.shape[-1]), flat)
    total = flat.shape[0] * lax.axis_size("gx") * lax.axis_size("gy")
    modes, mode, fac = k2(g, col, f, flat, float(total))
    return modes.reshape(basis.shape), mode.reshape(basis.shape[:-1]), fac


def solution(mesh):
    in_specs = (P(None, "gx", "gy", None), P(None, "gx", "gy", None, None), P())
    out_specs = (P(None, "gx", "gy", None, None), P(None, "gx", "gy", None), P())
    return jax.shard_map(local, mesh=mesh, in_specs=in_specs, out_specs=out_specs, check_vma=False)
```

```python
import functools
import jax, jax.numpy as jnp
from jax import lax
from jax.sharding import PartitionSpec as P
from jax.experimental import pallas as pl
from jax.experimental.pallas import tpu as pltpu

F32, BF16 = jnp.float32, jnp.bfloat16
B, H = 128, 64
HI = lax.Precision.HIGHEST


def lane_splat(tile, lane):
    return jnp.take_along_axis(tile, jnp.full((8, B), lane, jnp.int32), axis=1)


def row_splat(tile, row):
    return jnp.broadcast_to(tile[row:row + 1, :], (8, B))


def nn(x, y):
    return lax.dot_general(x, y, (((1,), (0,)), ((), ())), precision=HI, preferred_element_type=F32)


def tn(x, y):
    return lax.dot_general(x, y, (((0,), (0,)), ((), ())), precision=HI, preferred_element_type=F32)


def nt(x, y):
    return lax.dot_general(x, y, (((1,), (1,)), ((), ())), precision=HI, preferred_element_type=F32)


def nt16(x, y):
    return lax.dot_general(x, y, (((1,), (1,)), ((), ())), preferred_element_type=F32)


def split(x):
    hi = x.astype(BF16)
    return hi, (x - hi.astype(F32)).astype(BF16)


def factor_half(a, off, tick):
    sub = lax.broadcasted_iota(jnp.int32, (8, B), 0)
    lane = lax.broadcasted_iota(jnp.int32, (8, B), 1)
    mine = (lane >= H) if off else (lane < H)
    n = H // 8
    a = [jnp.where(mine, a[t], jnp.where(lane + off - H == 8 * t + sub, 1.0, 0.0)) for t in range(n)]
    diag = [lane_splat(a[0], off + j) for j in range(8)]
    for p in range(n):
        cols = diag
        below = range(p + 1, n)
        c = {t: [lane_splat(a[t], off + 8 * p + j) for j in range(8)] for t in below}
        if below:
            diag = [lane_splat(a[p + 1], off + 8 * (p + 1) + j) for j in range(8)]
        inv, row, mult = [], {}, {}
        pivots = jnp.ones((8, B), F32)
        pivot = row_splat(cols[0], 0)
        for k in range(8):
            pivots = jnp.where(sub == k, pivot, pivots)
            r = pl.reciprocal(pivot, approx=True)
            inv.append(r)
            m = cols[k] * r
            for j in range(k + 1, 8):
                row[k, j] = row_splat(cols[j], k)
            if k < 7:
                pivot = row_splat(cols[k + 1], k + 1) - (row[k, k + 1] * row[k, k + 1]) * r
                for j in range(k + 1, 8):
                    cols[j] = cols[j] - m * row[k, j]
                a[p] = a[p] - jnp.where(sub > k, m, 0.0) * row_splat(a[p], k)
        for t in below:
            for k in range(8):
                mult[t, k] = c[t][k] * inv[k]
                for j in range(k + 1, 8):
                    c[t][j] = c[t][j] - mult[t, k] * row[k, j]
        if below:
            for j in range(8):
                for k in range(8):
                    diag[j] = diag[j] - mult[p + 1, k] * row_splat(c[p + 1][k], j)
            for k in range(8):
                u = row_splat(a[p], k)
                for t in below:
                    a[t] = a[t] - mult[t, k] * u
        a[p] = a[p] * lax.rsqrt(pivots)
        tick()
    return jnp.concatenate(a, axis=0)


def factor_block(x, tick):
    lane = lax.broadcasted_iota(jnp.int32, (H, B), 1)
    rows = lax.broadcasted_iota(jnp.int32, (H, B), 0)
    low = lane < H
    zero = jnp.zeros((H, B), F32)
    p0 = factor_half([x[8 * t:8 * t + 8] for t in range(8)], 0, tick)
    r01 = nn(p0, jnp.concatenate([zero, jnp.where(low, 0.0, x[0:H])], axis=0))
    s11 = x[H:B] - tn(r01, r01)[H:B]
    w0 = jnp.where(low, pltpu.roll(p0, H, 1), 0.0)
    t10 = tn(r01, w0)[H:B]
    p1 = factor_half([s11[8 * t:8 * t + 8] for t in range(8)], H, tick)
    w10 = nn(p1, jnp.concatenate([t10, zero], axis=0))
    r = jnp.concatenate([jnp.where(low, jnp.where(lane >= rows, p0, 0.0), r01), jnp.where(lane >= rows + H, p1, 0.0)], axis=0)
    w = jnp.concatenate([w0, jnp.where(low, -w10, pltpu.roll(p1, H, 1))], axis=0)
    return r, w


OFF = [(b, c) for b in range(4) for c in range(b + 1, 4)]
PAIRS = [(b, c) for b in range(4) for c in range(b, 4)]
INDEX = {pair: i for i, pair in enumerate(PAIRS)}


def k2_kernel(total, g_ref, col_ref, f_ref, basis_hbm, modes_hbm, mode_hbm, factor_hbm, s_ref, zw_ref, zh_ref, zl_ref, basis_ref, modes_ref, factor_ref, v_ref, c_ref, mode_ref, load_s, out_s, fac_s):
    load = pltpu.make_async_copy(basis_hbm, basis_ref, load_s)
    load.start()
    scale = 1.0 / total
    brow = lax.broadcasted_iota(jnp.int32, (B, B), 0)
    bcol = lax.broadcasted_iota(jnp.int32, (B, B), 1)
    col = col_ref[...] * scale
    g8 = jnp.broadcast_to(jnp.concatenate([col[i:i + 1, :] for i in range(4)], axis=1), (8, 512))

    def stored(i):
        return jnp.concatenate([g_ref[4 * i + j] for j in range(4)], axis=0) * scale

    def unpack(i):
        both = stored(6 + i)
        flip = jnp.transpose(both)
        diag = jnp.broadcast_to(col[5 + i:6 + i, :], (B, B))
        s_ref[INDEX[2 * i + 1, 2 * i + 1]] = jnp.where(brow == bcol, diag, jnp.where(brow > bcol, both, flip))
        return jnp.where(brow <= bcol, both, flip)

    def unpack_last():
        s_ref[INDEX[2, 2]] = unpack(1)

    def keep(i):
        s_ref[INDEX[OFF[i]]] = stored(i)

    def clear(b):
        factor_ref[b * B:(b + 1) * B, 0:b * B] = jnp.zeros((B, b * B), F32)

    factor_ref[512:513, :] = jnp.zeros((1, 513), F32)
    v_ref[...] = jnp.zeros_like(v_ref)
    c_ref[...] = g8
    outs = []
    later = [functools.partial(keep, i) for i in range(6)] + [unpack_last] + [functools.partial(clear, b) for b in range(1, 4)]
    state = [jnp.zeros((8, 1), F32), None]

    def tick():
        if later:
            later.pop(0)()

    def start(src, dst, sem):
        outs.append(pltpu.make_async_copy(src, dst, sem))
        outs[-1].start()

    def panel(b, c):
        return factor_ref[b * B:(b + 1) * B, c * B:(c + 1) * B]

    def factor_off(b, c, w):
        factor_ref[b * B:(b + 1) * B, c * B:(c + 1) * B] = nn(w, s_ref[INDEX[b, c]])

    def inverse_row(b, w):
        lo, hi = b * B, (b + 1) * B
        if b:
            zw_ref[lo:hi, 0:lo] = nn(w, zw_ref[lo:hi, 0:lo])
        zw_ref[lo:hi, lo:hi] = w
        zh_ref[lo:hi, 0:hi], zl_ref[lo:hi, 0:hi] = split(zw_ref[lo:hi, 0:hi])

    def trail(b, i, c):
        s_ref[INDEX[i, c]] = s_ref[INDEX[i, c]] - tn(panel(b, i), panel(b, c))

    def inverse_trail(b, i):
        lo, hi = b * B, (b + 1) * B
        part = tn(panel(b, i), zw_ref[lo:hi, 0:hi])
        if b:
            zw_ref[i * B:(i + 1) * B, 0:lo] = zw_ref[i * B:(i + 1) * B, 0:lo] - part[:, 0:lo]
        zw_ref[i * B:(i + 1) * B, lo:hi] = -part[:, lo:hi]

    def column(b, w):
        lo, hi = b * B, (b + 1) * B
        c = c_ref[:, lo:hi]
        factor_ref[lo:hi, 512:513] = nt(w, c)[:, 0:1]
        start(factor_ref.at[pl.ds(lo, B)], factor_hbm.at[pl.ds(lo, B)], fac_s.at[b])
        r = nt(c, w)
        for i in range(b + 1, 4):
            c_ref[:, i * B:(i + 1) * B] = c_ref[:, i * B:(i + 1) * B] - nn(r, panel(b, i))
        state[0] = state[0] + jnp.sum(r * r, axis=1, keepdims=True)
        state[1] = r

    def back(b):
        hi = (b + 1) * B
        v_ref[:, 0:hi] = v_ref[:, 0:hi] + nn(state[1], zw_ref[b * B:hi, 0:hi])

    def apply(b, part):
        lo, hi = b * B, (b + 1) * B
        if b == 0 and part == 0:
            load.wait()
        top = part * (rows // 2)
        own = basis_ref[top:top + rows // 2, 0:hi]
        out = nt16(own, zh_ref[lo:hi, 0:hi]) + nt16(own, zl_ref[lo:hi, 0:hi])
        modes_ref[top:top + rows // 2, lo:hi] = out.astype(BF16)
        at = (pl.ds(top, rows // 2), pl.ds(lo, B))
        start(modes_ref.at[at], modes_hbm.at[at], out_s.at[2 * b + part])

    rows = basis_ref.shape[0]
    for b in range(4):
        lo, hi = b * B, (b + 1) * B
        r_own, w = factor_block(s_ref[INDEX[b, b]] if b else unpack(0), tick)
        while later:
            tick()
        if b < 3:
            factor_off(b, b + 1, w)
            trail(b, b + 1, b + 1)
        factor_ref[lo:hi, lo:hi] = r_own
        for c in range(b + 2, 4):
            later.append(functools.partial(factor_off, b, c, w))
        later.append(functools.partial(column, b, w))
        later.append(functools.partial(inverse_row, b, w))
        later.append(functools.partial(back, b))
        for i in range(b + 1, 4):
            for c in range(i, 4):
                if (i, c) != (b + 1, b + 1):
                    later.append(functools.partial(trail, b, i, c))
            later.append(functools.partial(inverse_trail, b, i))
        later.append(functools.partial(apply, b, 0))
        later.append(functools.partial(apply, b, 1))
    while later:
        tick()
    v, norm = v_ref[...], state[0]
    d2 = col[4:5, 0:1] - norm[0:1]
    inv_d = lax.rsqrt(d2)
    factor_ref[512:513, 512:513] = d2 * inv_d
    outs.append(pltpu.make_async_copy(factor_ref.at[pl.ds(512, 1)], factor_hbm.at[pl.ds(512, 1)], fac_s.at[4]))
    outs[-1].start()
    vh, vl = split(v)
    y = nt16(vh, basis_ref[...]) + nt16(vl, basis_ref[...])
    f = f_ref[...]
    for i in range(6):
        mode_ref[i // 2, i % 2:i % 2 + 1, :] = (f[i:i + 1, :] - y[0:1, i * B:(i + 1) * B]) * inv_d
    start(mode_ref, mode_hbm, fac_s.at[5])
    for c in outs:
        c.wait()


def k2(g, col, f, basis, total):
    rows = basis.shape[0]
    vmem, hbm, dma = pltpu.VMEM, pltpu.HBM, pltpu.SemaphoreType.DMA
    return pl.pallas_call(
        functools.partial(k2_kernel, total),
        out_shape=(jax.ShapeDtypeStruct((rows, 512), BF16), jax.ShapeDtypeStruct((3, 2, B), F32), jax.ShapeDtypeStruct((513, 513), F32)),
        in_specs=[pl.BlockSpec(memory_space=vmem)] * 3 + [pl.BlockSpec(memory_space=hbm)],
        out_specs=[pl.BlockSpec(memory_space=hbm)] * 3,
        scratch_shapes=[
            vmem((10, B, B), F32), vmem((512, 512), F32), vmem((512, 512), BF16), vmem((512, 512), BF16),
            vmem((rows, 512), BF16), vmem((rows, 512), BF16), vmem((513, 513), F32), vmem((8, 512), F32), vmem((8, 512), F32), vmem((3, 2, B), F32), dma, dma((8,)), dma((6,)),
        ],
        compiler_params=pltpu.CompilerParams(vmem_limit_bytes=40 << 20),
        name="factor",
    )(g, col, f, basis)

MESH = pl.DeviceIdType.MESH
NPLANE, NZR, CH = 16, 16, 32
PIECE = CH // NZR
NEAR = [(dx, dy) for dx in (0, 1, -1) for dy in (0, 1, -1) if (dx, dy) != (0, 0)]
AROUND = sorted(((dx, dy) for dx in range(4) for dy in range(4) if dx or dy), key=lambda o: -(min(o[0], 4 - o[0]) + min(o[1], 4 - o[1])))
ALONG = sorted(range(1, NZR), key=lambda k: -min(k, NZR - k))


def tap_tiles(taps, d, sub):
    def at(i):
        return jnp.broadcast_to(taps[d:d + 1, i:i + 1], (8, B))
    ahead = behind = jnp.zeros((8, B), F32)
    for s in range(8):
        ahead = jnp.where(sub == s, at(8 + s), ahead)
        behind = jnp.where(sub == s, at(s), behind)
    return ahead, behind, jnp.where(sub == 0, at(16), 0.0)


def reduce_kernel(taps_hbm, snap_hbm, basis_hbm, full_ref, col_ref, filt_ref, taps_ref, snap_ref, basis_ref, band_ref, near_out, near_in, acc, recv_a, recv_b, chunk_ref, recv_c, piece_ref, ring_ref, whole_ref, gsend, grecv, gsib, gin, gout, gz, load_s, near_s, near_r, sa, ra, sb, rb, sc, rc, sd, rd, se, re, sf, rf, sga, rga, sgb, rgb, sgc, rgc, second, third):
    gx, gy = lax.axis_index("gx"), lax.axis_index("gy")
    x, z = gx // NZR, gx % NZR
    y, core = gy // 2, gy % 2
    plane = x * 4 + y

    def near_id(dx, dy):
        return ((gx + dx + 64) % 64, (gy + dy + 8) % 8)

    def plane_at(o):
        return ((x + o[0]) % 4) * 4 + (y + o[1]) % 4

    def plane_id(o):
        return (((x + o[0]) % 4) * NZR + z, ((y + o[1]) % 4) * 2 + core)

    def z_id(k):
        return (x * NZR + (z + k) % NZR, gy)

    sibling = (gx, y * 2 + (1 - core))
    barrier = pltpu.get_barrier_semaphore()
    partners = [sibling] + [plane_id(o) for o in AROUND if 0 in o] + [z_id(k) for k in (1, 2, NZR - 2, NZR - 1)]
    for partner in partners:
        pl.semaphore_signal(barrier, inc=1, device_id=partner, device_id_type=MESH)
    loads = []
    for i in range(3):
        loads.append(pltpu.make_async_copy(basis_hbm.at[pl.ds(256 * i, 256)], basis_ref.at[pl.ds(256 * i, 256)], load_s.at[4 + i]))
    loads.append(pltpu.make_async_copy(taps_hbm, taps_ref, load_s.at[0]))
    for i in range(3):
        loads.append(pltpu.make_async_copy(snap_hbm.at[pl.ds(128 * i, 128)], snap_ref.at[pl.ds(128 * i, 128)], load_s.at[1 + i]))
    for c in loads:
        c.start()

    sub = lax.broadcasted_iota(jnp.int32, (8, B), 0)
    lane = lax.broadcasted_iota(jnp.int32, (8, B), 1)
    for c in loads[:3]:
        c.wait()
    own = {}
    for b in range(4):
        part = lax.dot_general(basis_ref[:, b * B:(b + 1) * B], basis_ref[:, b * B:512], (((0,), (0,)), ((), ())), preferred_element_type=F32)
        for c in range(b, 4):
            if c == b:
                own[b] = part[:, 0:B]
            else:
                at = OFF.index((b, c)) * B
                acc[at:at + B, :] = part[:, (c - b) * B:(c - b + 1) * B]
    brow = lax.broadcasted_iota(jnp.int32, (B, B), 0)
    bcol = lax.broadcasted_iota(jnp.int32, (B, B), 1)
    for i in range(2):
        acc[768 + i * B:896 + i * B, :] = jnp.where(brow <= bcol, own[2 * i], own[2 * i + 1])
    diag = [jnp.sum(jnp.where(brow == bcol, own[i], 0.0), axis=0, keepdims=True) for i in (1, 3)]
    pl.semaphore_wait(barrier, len(partners))
    for partner in partners:
        pl.semaphore_signal(second, inc=1, device_id=partner, device_id_type=MESH)

    def copy(src, dst, ssem, rsem, device):
        c = pltpu.make_async_remote_copy(src_ref=src, dst_ref=dst, send_sem=ssem, recv_sem=rsem, device_id=device, device_id_type=MESH)
        c.start()
        return c

    half = NPLANE * CH
    ca = copy(acc.at[pl.ds((1 - core) * half, half)], recv_a, sa, ra, sibling)
    loads[3].wait()
    taps = taps_ref[...].astype(F32)
    ahead, behind, last = tap_tiles(taps, 2, sub)
    for m in range(0, 128, 2):
        pair = []
        for t in (m, m + 1):
            tile = jnp.where(lane == t, ahead, 0.0)
            tile = jnp.where(lane == (t + 1) % 128, behind, tile)
            pair.append(jnp.where(lane == (t + 127) % 128, last, tile))
        band_ref[8 * m:8 * m + 16, :] = jnp.concatenate(pair, axis=0).astype(BF16)
    for c in loads[4:]:
        c.wait()
    along_z = jnp.dot(snap_ref[...], band_ref[...], preferred_element_type=F32)
    ahead, behind, last = tap_tiles(taps, 0, sub)
    w_ahead = [row_splat(ahead, s) for s in range(8)]
    w_behind = [row_splat(behind, s) for s in range(8)]
    w_last = row_splat(last, 0)
    ahead, behind, last = tap_tiles(taps, 1, sub)
    sums = {}
    for dx in (0, 1, -1):
        for dy in (0, 1, -1):
            sums[dx, dy] = jnp.zeros((8, B), F32)
    for c in range(3):
        cell = [[along_z[(c * 8 + i) * 16 + 8 * h:(c * 8 + i) * 16 + 8 * h + 8, :] for i in range(8)] for h in range(2)]
        for dx in (0, 1, -1):
            part = []
            for h in range(2):
                if dx == -1:
                    part.append(w_last * cell[h][0])
                else:
                    w = w_ahead if dx == 0 else w_behind
                    v = w[0] * cell[h][0]
                    for i in range(1, 8):
                        v = v + w[i] * cell[h][i]
                    part.append(v)
            def put(dy, q, tile):
                total = jnp.sum(tile, axis=0, keepdims=True)
                sums[dx, dy] = jnp.where(sub == 2 * c + q, jnp.broadcast_to(total, (8, B)), sums[dx, dy])
            put(0, 0, ahead * part[0] + last * part[1])
            put(0, 1, behind * part[0] + ahead * part[1])
            put(1, 0, behind * part[1])
            put(-1, 1, last * part[0])
    for e, (dx, dy) in enumerate(NEAR):
        tile = sums[dx, dy]
        if dy == 1:
            tile = jnp.where(gy == 7, 0.0, tile)
        if dy == -1:
            tile = jnp.where(gy == 0, 0.0, tile)
        near_out[e] = tile
    pl.semaphore_wait(second, len(partners))
    third_id = [z_id(4), z_id(NZR - 4), near_id(1, 0), near_id(-1, 0)]
    for partner in third_id:
        pl.semaphore_signal(third, inc=1, device_id=partner, device_id_type=MESH)
    ca.wait_recv()
    def halved(p):
        rows = pl.ds(p * CH, CH)
        recv_a[rows, :] = recv_a[rows, :] + acc[pl.ds(core * half + p * CH, CH), :]
    cb = []
    for e, o in enumerate(AROUND):
        p = plane_at(o)
        halved(p)
        cb.append(copy(recv_a.at[pl.ds(p * CH, CH)], recv_b.at[e], sb.at[e], rb.at[e], plane_id(o)))
    halved(plane)
    pl.semaphore_wait(third, len(third_id))
    near = [copy(near_out.at[e], near_in.at[e], near_s.at[e], near_r.at[e], near_id(dx, dy)) for e, (dx, dy) in enumerate(NEAR)]
    total = recv_a[pl.ds(plane * CH, CH), :]
    for e in reversed(range(NPLANE - 1)):
        cb[e].wait_recv()
        total = total + recv_b[e]
    for i in range(NZR):
        chunk_ref[i] = total[i * PIECE:(i + 1) * PIECE, :]
    cc = []
    for e, k in enumerate(ALONG):
        cc.append(copy(chunk_ref.at[(z + k) % NZR], recv_c.at[e], sc.at[e], rc.at[e], z_id(k)))
    for c in near:
        c.wait_recv()
    f = sums[0, 0]
    for e in range(len(NEAR)):
        f = f + near_in[e]
    f16 = f.astype(BF16)
    f = f16.astype(F32)
    filt_ref[...] = f[0:6, :]
    frow = jnp.concatenate([jnp.broadcast_to(f[i:i + 1, :], (8, B)) for i in range(6)], axis=1).astype(BF16)
    g = jnp.dot(frow, basis_ref[...], preferred_element_type=F32)
    sq = jnp.where(sub < 6, f * f, 0.0)
    ff = jnp.sum(jnp.sum(sq, axis=1, keepdims=True), axis=0, keepdims=True)
    tail = jnp.where(sub == 4, jnp.broadcast_to(ff, (8, B)), 0.0)
    for i in range(2):
        tail = jnp.where(sub == 5 + i, jnp.broadcast_to(diag[i], (8, B)), tail)
    for i in range(4):
        tail = jnp.where(sub == i, g[:, i * B:(i + 1) * B], tail)
    gsend[...] = tail
    cga = copy(gsend, gsib, sga, rga, sibling)
    cga.wait_recv()
    gin[plane] = tail + gsib[...]
    cgb = [copy(gin.at[plane], gin.at[plane], sgb.at[e], rgb.at[e], plane_id(o)) for e, o in enumerate(AROUND)]
    total = chunk_ref[z]
    for e in reversed(range(NZR - 1)):
        cc[e].wait_recv()
        total = total + recv_c[e]
    piece_ref[...] = total
    cd = []
    for e, k in enumerate(ALONG):
        cd.append(copy(piece_ref, ring_ref.at[z], sd.at[e], rd.at[e], z_id(k)))
    ring_ref[z] = total
    for c in reversed(cgb):
        c.wait_recv()
    column = gin[0]
    for i in range(1, NPLANE):
        column = column + gin[i]
    gout[...] = column
    gz[z] = column
    cgc = [copy(gout, gz.at[z], sgc.at[e], rgc.at[e], z_id(k)) for e, k in enumerate(ALONG)]
    for c in reversed(cd):
        c.wait_recv()
    for i in range(NZR):
        whole_ref[i * PIECE:(i + 1) * PIECE, :] = ring_ref[i]
    rows = pl.ds(0, CH)
    def slot(c, p):
        return full_ref.at[c * NPLANE + p, rows]
    ce = []
    for e, o in enumerate(AROUND):
        ce.append(copy(whole_ref.at[rows], slot(core, plane), se.at[e], re.at[e], plane_id(o)))
    cf = [copy(whole_ref.at[rows], slot(core, plane), sf.at[NPLANE - 1], rf.at[NPLANE - 1], sibling)]
    full_ref[core * NPLANE + plane] = whole_ref[...]
    for e in reversed(range(NPLANE - 1)):
        ce[e].wait_recv()
        p = plane_at((4 - AROUND[e][0], 4 - AROUND[e][1]))
        cf.append(copy(slot(core, p), slot(core, p), sf.at[e], rf.at[e], sibling))
    for c in reversed(cgc):
        c.wait_recv()
    column = gz[0]
    for i in range(1, NZR):
        column = column + gz[i]
    col_ref[...] = column
    for c in cf:
        c.wait_recv()
    for c in near + [ca, cga] + cb + cgb + cc + cd + cgc + ce + cf:
        c.wait_send()


def reduced(taps, snap, basis):
    dma = pltpu.SemaphoreType.DMA
    vmem = pltpu.VMEM
    n = NPLANE - 1
    return pl.pallas_call(
        reduce_kernel,
        out_shape=(jax.ShapeDtypeStruct((2 * NPLANE, CH, B), F32), jax.ShapeDtypeStruct((8, B), F32), jax.ShapeDtypeStruct((6, B), F32)),
        in_specs=[pl.BlockSpec(memory_space=pltpu.HBM)] * 3,
        out_specs=[pl.BlockSpec(memory_space=vmem)] * 3,
        scratch_shapes=[
            vmem((3, 17), BF16),
            vmem((384, 1024), BF16),
            vmem((768, 512), BF16),
            vmem((1024, B), BF16),
            vmem((8, 8, B), F32),
            vmem((8, 8, B), F32),
            vmem((2 * NPLANE * CH, B), F32),
            vmem((NPLANE * CH, B), F32),
            vmem((n, CH, B), F32),
            vmem((NZR, PIECE, B), F32),
            vmem((n, PIECE, B), F32),
            vmem((PIECE, B), F32),
            vmem((NZR, PIECE, B), F32),
            vmem((CH, B), F32),
            vmem((8, B), F32),
            vmem((8, B), F32),
            vmem((8, B), F32),
            vmem((NPLANE, 8, B), F32),
            vmem((8, B), F32),
            vmem((NZR, 8, B), F32),
            dma((7,)), dma((8,)), dma((8,)), dma, dma,
            dma((n,)), dma((n,)), dma((n,)), dma((n,)), dma((n,)), dma((n,)), dma((n,)), dma((n,)), dma((n + 1,)), dma((n + 1,)),
            dma, dma, dma((n,)), dma((n,)), dma((n,)), dma((n,)), pltpu.SemaphoreType.REGULAR, pltpu.SemaphoreType.REGULAR,
        ],
        compiler_params=pltpu.CompilerParams(vmem_limit_bytes=40<<20, collective_id=0, has_side_effects=True),
        name="reduce",
    )(pltpu.with_memory_space_constraint(taps, pltpu.HBM), pltpu.with_memory_space_constraint(snap, pltpu.HBM), basis)


def local(snapshot, basis, taps):
    flat = pltpu.with_memory_space_constraint(basis.reshape(-1, basis.shape[-1]), pltpu.HBM)
    g, col, f = reduced(taps, snapshot.reshape(-1, snapshot.shape[-1]), flat)
    total = flat.shape[0] * lax.axis_size("gx") * lax.axis_size("gy")
    modes, mode, fac = k2(g, col, f, flat, float(total))
    return modes.reshape(basis.shape), mode.reshape(basis.shape[:-1]), fac


def solution(mesh):
    in_specs = (P(None, "gx", "gy", None), P(None, "gx", "gy", None, None), P())
    out_specs = (P(None, "gx", "gy", None, None), P(None, "gx", "gy", None), P())
    return jax.shard_map(local, mesh=mesh, in_specs=in_specs, out_specs=out_specs, check_vma=False)
```
